512 devices in a mesh: seq: 16 (over z, y_hi), res: 32 (over y_lo, x, core).
Axes of the slice: x: 4, y: 8 (y_hi: 2, y_lo: 4; y = y_hi * 4 + y_lo), z: 8, core: 2. Of those that a mesh axis runs over, the one named last changes fastest.
Arguments:
- queries: bfloat16 [64, 2048, 384], P('seq', 'res'), may hold values from -64 to 64
- keys: bfloat16 [64, 2048, 384], P('seq', 'res'), may hold values from -4 to 4
- values: bfloat16 [64, 2048, 384], P('seq', 'res'), may hold values from -6 to 6
Outputs:
- attended: bfloat16 [64, 2048, 384], P('seq', 'res')
The draws below stay inside these ranges and needn't reach their ends.
All inputs are finite; a program needn't handle non-finite values.
Results may differ from the reference program's by a relative error of at most 0.0049.
Values may be sent and summed in bfloat16 or wider, within the bound.
A program may use at most 64 MiB of HBM per device.

```python
import jax
import jax.numpy as jnp
from jax import lax

HEADS = 6
D = 384
ALIGNED_SEQS = 64
RESIDUE_COLUMNS = 2048


def base_keys(key):
    return jnp.clip(jax.random.normal(key, (ALIGNED_SEQS, RESIDUE_COLUMNS, D), jnp.float32), -4.0, 4.0)


def draw_keys(key, part):
    shared = base_keys(key)
    return shared.astype(jnp.bfloat16)


def draw_queries(key, part):
    key = jax.random.fold_in(key, 7)
    drawn = jnp.clip(jax.random.normal(key, (ALIGNED_SEQS, RESIDUE_COLUMNS, D), jnp.float32), -4.0, 4.0)
    return drawn.astype(jnp.bfloat16)


def shard_levels(rng, dims, cuts, least, largest):
    def one(axis_at, shards_of):
        steps = jax.random.uniform(jax.random.fold_in(jax.random.fold_in(rng, 6), axis_at), (shards_of,), jnp.float32, least / len(cuts), largest / len(cuts))
        return jnp.repeat(jnp.exp(steps), dims[axis_at] // shards_of).reshape((-1,) + (1,) * (len(dims) - axis_at - 1))

    loudness = one(*cuts[0])
    for cut in cuts[1:]:
        loudness = loudness * one(*cut)
    return loudness


def bell_draw(stream_key, dims, width, bound, pieces=(), kind=jnp.bfloat16):
    values = jax.random.normal(stream_key, dims, jnp.float32) * width
    if len(pieces) > 0:
        values = shard_levels(stream_key, dims, pieces, -0.22, 0.18) * values
    return jnp.clip(values, min=-bound, max=bound).astype(kind)


def setup_inputs(seed: int = 0) -> dict:
    key_of = jax.random.split(jax.random.key(seed), 4)
    return {
        "queries": draw_queries(jax.random.fold_in(key_of[3], 71), 0),
        "keys": draw_keys(jax.random.fold_in(key_of[3], 71), 0),
        "values": bell_draw(key_of[2], (ALIGNED_SEQS, RESIDUE_COLUMNS, D), 1.0, 6.0, ((0, 16), (1, 32))),
    }


def reference(queries, keys, values):
    head_index = D // HEADS
    scale = (head_index ** -0.5) / (ALIGNED_SEQS ** 0.5)
    q4 = queries.reshape(ALIGNED_SEQS, RESIDUE_COLUMNS, HEADS, head_index)
    k4 = keys.reshape(ALIGNED_SEQS, RESIDUE_COLUMNS, HEADS, head_index)
    value_tensor_four = values.reshape(ALIGNED_SEQS, RESIDUE_COLUMNS, HEADS, head_index)

    def one_head(position_index):
        qmat = lax.dynamic_index_in_dim(q4, position_index, 2, keepdims=False)
        kmat = lax.dynamic_index_in_dim(k4, position_index, 2, keepdims=False)
        value_matrix = lax.dynamic_index_in_dim(value_tensor_four, position_index, 2, keepdims=False)
        qflat = jnp.transpose(qmat, (1, 0, 2)).reshape(RESIDUE_COLUMNS, ALIGNED_SEQS * head_index)
        kflat = jnp.transpose(kmat, (1, 0, 2)).reshape(RESIDUE_COLUMNS, ALIGNED_SEQS * head_index)
        value_flattened = jnp.transpose(value_matrix, (1, 0, 2)).reshape(RESIDUE_COLUMNS, ALIGNED_SEQS * head_index)
        scores = jnp.dot(qflat, kflat.T, preferred_element_type=jnp.float32) * scale
        probs = jax.nn.softmax(scores, axis=-1).astype(jnp.bfloat16)
        mixed = jnp.dot(probs, value_flattened, preferred_element_type=jnp.float32)
        return mixed.astype(jnp.bfloat16).reshape(RESIDUE_COLUMNS, ALIGNED_SEQS, head_index)

    stacked = lax.map(one_head, jnp.arange(HEADS, dtype=jnp.int32))
    return jnp.transpose(stacked, (2, 1, 0, 3)).reshape(ALIGNED_SEQS, RESIDUE_COLUMNS, D)
```

```python
import functools

import jax
import jax.numpy as jnp
from jax import lax
from jax.experimental import pallas as pl
from jax.experimental.pallas import tpu as pltpu
from jax.sharding import PartitionSpec as P

NZ, NY, NX = 8, 8, 4
PAIRS = 3
ROWS, TOK, LANES = 4, 64, 128
F32, BF16 = jnp.float32, jnp.bfloat16


def kernel(
    q_hbm, k_hbm, v_hbm, out_hbm,
    kbuf, vbuf, qbuf, qsend, qm, kcat, sbuf, zrecv, stat, statv, pbuf, obuf, orecv, xrecv, oown, oswap,
    load_sem, out_sem, k_ss, k_rs, v_ss, v_rs, qs_ss, qs_rs, qx_ss, qx_rs, z_ss, z_rs, st_ss, st_rs,
    p_ss, p_rs, o_ss, o_rs, x_ss, x_rs, w_ss, w_rs,
):
    s_id, r_id = lax.axis_index("seq"), lax.axis_index("res")
    z, yh = s_id // 2, s_id % 2
    yl, x, c = r_id // 8, (r_id // 2) % 4, r_id % 2
    y = yh * 4 + yl

    def at(z_=None, y_=None, x_=None, c_=None):
        z_ = z if z_ is None else z_
        y_ = y if y_ is None else y_
        x_ = x if x_ is None else x_
        c_ = c if c_ is None else c_
        return {"seq": z_ * 2 + y_ // 4, "res": ((y_ % 4) * 4 + x_) * 2 + c_}

    def zdev(k):
        return at(z_=(z + k + NZ) % NZ)

    def ydev(k):
        return at(y_=(y + k + NY) % NY)

    partner = at(y_=(y + 4) % NY, c_=1 - c)
    sibling = at(c_=1 - c)

    def group(k):
        g = (x * 2 + c + k) % 8
        return at(x_=g // 2, c_=g % 2)

    def group_index(k):
        g = (x * 2 + c + k + 8) % 8
        return g // 2, g % 2

    def remote(src, dst, ss, rs, dev):
        return pltpu.make_async_remote_copy(
            src_ref=src, dst_ref=dst, send_sem=ss, recv_sem=rs, device_id=dev, device_id_type=pl.DeviceIdType.MESH
        )

    home = c == yh

    def lanes(p):
        return pl.ds(p * LANES, LANES)

    def load_k(p):
        return pltpu.make_async_copy(k_hbm.at[:, :, lanes(p)], kbuf.at[p, y], load_sem.at[0, p])

    def load_v(p):
        return pltpu.make_async_copy(v_hbm.at[:, :, lanes(p)], vbuf.at[p, y], load_sem.at[1, p])

    def load_q_home(p):
        return pltpu.make_async_copy(q_hbm.at[:, :, lanes(p)], qbuf.at[p, c, x], load_sem.at[2, p])

    def load_q_away(p):
        return pltpu.make_async_copy(q_hbm.at[:, :, lanes(p)], qsend.at[p], load_sem.at[2, p])

    def ring(buf, ss, rs, p, step, way):
        src = (y - way * (step - 1) + NY) % NY
        half = pl.ds(0, ROWS) if step < 4 else (pl.ds(0, 2) if way == 1 else pl.ds(2, 2))
        d = 0 if way == 1 else 1
        view = buf.at[p, src, half]
        return remote(view, view, ss.at[p, step - 1, d], rs.at[p, step - 1, d], ydev(way))

    def ring_recv(buf, ss, rs, p, step, way):
        src = (y - way * step + NY) % NY
        half = pl.ds(0, ROWS) if step < 4 else (pl.ds(0, 2) if way == 1 else pl.ds(2, 2))
        d = 0 if way == 1 else 1
        view = buf.at[p, src, half]
        return remote(view, view, ss.at[p, step - 1, d], rs.at[p, step - 1, d], ydev(way))

    def ring_start(buf, ss, rs, p, step):
        for way in (1, -1):
            ring(buf, ss, rs, p, step, way).start()

    def ring_wait(buf, ss, rs, p, step):
        for way in (1, -1):
            ring_recv(buf, ss, rs, p, step, way).wait_recv()

    def ring_end(buf, ss, rs, p):
        for step in range(1, 5):
            for way in (1, -1):
                ring(buf, ss, rs, p, step, way).wait_send()

    K = (kbuf, k_ss, k_rs)
    V = (vbuf, v_ss, v_rs)

    def q_swap(p):
        return remote(qsend.at[p], qbuf.at[p, 1 - c, x], qs_ss.at[p], qs_rs.at[p], partner)

    def q_swap_recv(p):
        return remote(qsend.at[p], qbuf.at[p, c, x], qs_ss.at[p], qs_rs.at[p], partner)

    def q_ready(p):
        @pl.when(home)
        def _():
            load_q_home(p).wait()

        @pl.when(jnp.logical_not(home))
        def _():
            q_swap_recv(p).wait_recv()

    def q_spread(p, k):
        view = qbuf.at[p, c, x]
        return remote(view, view, qx_ss.at[p, k - 1], qx_rs.at[p, k - 1], group(k))

    def q_spread_recv(p, k):
        gx, gc = group_index(-k)
        view = qbuf.at[p, gc, gx]
        return remote(view, view, qx_ss.at[p, k - 1], qx_rs.at[p, k - 1], group(k))

    lane = lax.broadcasted_iota(jnp.int32, (256, LANES), 1)

    def scores(p):
        for g in range(2):
            for r in range(ROWS):
                cols = pl.ds((g * ROWS + r) * LANES, LANES)
                block = qbuf[p, g, :, r].reshape(256, LANES)
                zero = jnp.zeros_like(block)
                qm[0:256, cols] = jnp.where(lane < 64, block, zero)
                qm[256:512, cols] = jnp.where(lane >= 64, block, zero)
                kcat[:, cols] = kbuf[p, g * 4 : g * 4 + 4, r].reshape(256, LANES)
        for half in range(2):
            part = lax.dot_general(
                qm[half * 256 : half * 256 + 256, :], kcat[...], (((1,), (1,)), ((), ())), preferred_element_type=F32
            )
            sbuf[p, half * 4 : half * 4 + 4] = part.reshape(4, TOK, 256)

    def zslice(way, step):
        return (z + way * (5 - step) + NZ) % NZ

    def z_copy(p, step, way):
        d = 0 if way == 1 else 1
        half = pl.ds(0, TOK) if step > 1 else pl.ds(d * 32, 32)
        return remote(
            sbuf.at[p, zslice(way, step), half],
            zrecv.at[p, d, step - 1, half],
            z_ss.at[p, step - 1, d],
            z_rs.at[p, step - 1, d],
            zdev(way),
        )

    def z_start(p, step):
        for way in (1, -1):
            z_copy(p, step, way).start()

    def z_add(p, step):
        for way in (1, -1):
            d = 0 if way == 1 else 1
            z_copy(p, step, way).wait_recv()
            s = zslice(way, step + 1)
            if step == 1:
                rows = pl.ds(d * 32, 32)
                sbuf[p, s, rows] = sbuf[p, s, rows] + zrecv[p, d, 0, rows]
            else:
                sbuf[p, s] = sbuf[p, s] + zrecv[p, d, step - 1]

    def stat_copy(p, k):
        return remote(stat.at[p, 0], stat.at[p, k], st_ss.at[p, k - 1], st_rs.at[p, k - 1], group(k))

    def softmax_local(p):
        for way in (1, -1):
            z_copy(p, 4, way).wait_recv()
        s = sbuf[p, z] + zrecv[p, 0, 3] + zrecv[p, 1, 3]
        s = s * (1.0 / 64.0)
        m = jnp.max(s, axis=1, keepdims=True)
        e = jnp.exp(s - m)
        l = jnp.sum(e, axis=1, keepdims=True)
        statv[p] = e
        col = lax.broadcasted_iota(jnp.int32, (TOK, LANES), 1)
        both = jnp.where(col == 0, m, l)
        tall = jnp.concatenate([both, both], axis=0)
        stat[p, 0] = jnp.transpose(tall)[0:8, :]
        for k in range(1, 8):
            stat_copy(p, k).start()

    def softmax_global(p):
        for k in range(1, 8):
            stat_copy(p, k).wait_recv()
        m = stat[p, 0, 0:1, :]
        for k in range(1, 8):
            m = jnp.maximum(m, stat[p, k, 0:1, :])
        l = jnp.zeros_like(m)
        for k in range(8):
            l = l + jnp.exp(stat[p, k, 0:1, :] - m) * stat[p, k, 1:2, :]
        factor = jnp.exp(stat[p, 0, 0:1, :] - m) / l
        tall = jnp.transpose(jnp.broadcast_to(factor, (LANES, LANES)))
        pbuf[p, z] = (statv[p] * tall[0:TOK, 0:1]).astype(BF16)
        for k in range(1, 8):
            p_copy(p, k).start()

    def p_copy(p, k):
        return remote(pbuf.at[p, z], pbuf.at[p, z], p_ss.at[p, k - 1], p_rs.at[p, k - 1], zdev(k))

    def p_recv(p, k):
        view = pbuf.at[p, (z - k + NZ) % NZ]
        return remote(view, view, p_ss.at[p, k - 1], p_rs.at[p, k - 1], zdev(k))

    def attend(p, g):
        probs = pbuf[p].reshape(512, 256)
        for r in range(0, ROWS, 2):
            vals = jnp.concatenate([vbuf[p, pl.ds(g * 4, 4), r + i].reshape(256, LANES) for i in range(2)], axis=1)
            o = lax.dot_general(probs, vals, (((1,), (0,)), ((), ())), preferred_element_type=F32)
            for i in range(2):
                cols = slice(i * LANES, (i + 1) * LANES)
                both = jnp.where(lane < 64, o[0:256, cols], o[256:512, cols])
                obuf[p, g, :, r + i] = both.reshape(NX, TOK, LANES)

    def o_copy(p):
        return remote(obuf.at[p, 1 - c], orecv.at[p], o_ss.at[p], o_rs.at[p], sibling)

    def x_copy(p, k):
        to = (x + k) % NX
        return remote(obuf.at[p, c, to], xrecv.at[p, k - 1], x_ss.at[p, k - 1], x_rs.at[p, k - 1], at(x_=to))

    def attend_all(p):
        for k in range(1, 8):
            p_recv(p, k).wait_recv()
        attend(p, 1 - c)
        o_copy(p).start()
        attend(p, c)

    def chip_sum(p):
        o_copy(p).wait_recv()
        for k in (2, 1, 3):
            to = (x + k) % NX
            obuf[p, c, to] = obuf[p, c, to] + orecv[p, to]
            x_copy(p, k).start()

    def out_home(p):
        return pltpu.make_async_copy(oown.at[p], out_hbm.at[:, :, lanes(p)], out_sem.at[p])

    def out_away(p):
        return pltpu.make_async_copy(oswap.at[p], out_hbm.at[:, :, lanes(p)], out_sem.at[p])

    def w_copy(p):
        return remote(oown.at[p], oswap.at[p], w_ss.at[p], w_rs.at[p], partner)

    def finish(p):
        total = obuf[p, c, x] + orecv[p, x]
        for k in (1, 2, 3):
            x_copy(p, k).wait_recv()
        total = total + xrecv[p, 0] + xrecv[p, 1] + xrecv[p, 2]
        oown[p] = total.astype(BF16)

        @pl.when(home)
        def _():
            out_home(p).start()

        @pl.when(jnp.logical_not(home))
        def _():
            w_copy(p).start()

    for p in range(PAIRS):
        load_k(p).start()

        @pl.when(home)
        def _():
            load_q_home(p).start()

        @pl.when(jnp.logical_not(home))
        def _():
            load_q_away(p).start()

    for p in range(PAIRS):
        load_v(p).start()

    barrier = pltpu.get_barrier_semaphore()
    peers = [zdev(k) for k in range(1, 8)] + [ydev(1), ydev(-1), partner] + [group(k) for k in range(1, 8)]
    for dev in peers:
        pl.semaphore_signal(barrier, inc=1, device_id=dev, device_id_type=pl.DeviceIdType.MESH)
    pl.semaphore_wait(barrier, len(peers))

    for p in range(PAIRS):
        load_k(p).wait()
        ring_start(*K, p, 1)

        @pl.when(jnp.logical_not(home))
        def _():
            load_q_away(p).wait()
            q_swap(p).start()

    for p in range(PAIRS):
        ring_wait(*K, p, 1)
        ring_start(*K, p, 2)
    for p in range(PAIRS):
        q_ready(p)
        for k in range(1, 8):
            q_spread(p, k).start()
    for p in range(PAIRS):
        ring_wait(*K, p, 2)
        ring_start(*K, p, 3)
    for p in range(PAIRS):
        ring_wait(*K, p, 3)
        ring_start(*K, p, 4)
    for p in range(PAIRS):
        load_v(p).wait()
        ring_start(*V, p, 1)
    for p in range(PAIRS):
        ring_wait(*K, p, 4)
        for k in range(1, 8):
            q_spread_recv(p, k).wait_recv()
        scores(p)
        z_start(p, 1)
    for step in (1, 2, 3):
        for p in range(PAIRS):
            z_add(p, step)
            z_start(p, step + 1)
        for p in range(PAIRS):
            ring_wait(*V, p, step)
            ring_start(*V, p, step + 1)
    for p in range(PAIRS):
        softmax_local(p)
    for p in range(PAIRS):
        softmax_global(p)
    for p in range(PAIRS):
        ring_wait(*V, p, 4)
    for p in range(PAIRS):
        attend_all(p)
        chip_sum(p)
    for p in range(PAIRS):
        finish(p)

    for p in range(PAIRS):
        @pl.when(home)
        def _():
            out_home(p).wait()

        @pl.when(jnp.logical_not(home))
        def _():
            w_copy(p).wait_recv()
            out_away(p).start()
            q_swap(p).wait_send()
            w_copy(p).wait_send()
            out_away(p).wait()

        ring_end(*K, p)
        ring_end(*V, p)
        for k in range(1, 8):
            q_spread(p, k).wait_send()
            stat_copy(p, k).wait_send()
            p_copy(p, k).wait_send()
        for step in range(1, 5):
            for way in (1, -1):
                z_copy(p, step, way).wait_send()
        o_copy(p).wait_send()
        for k in (1, 2, 3):
            x_copy(p, k).wait_send()


def local(queries, keys, values):
    vmem = pltpu.VMEM
    dma = pltpu.SemaphoreType.DMA
    block = (ROWS, TOK, LANES)
    return pl.pallas_call(
        kernel,
        out_shape=jax.ShapeDtypeStruct(queries.shape, BF16),
        in_specs=[pl.BlockSpec(memory_space=pl.ANY)] * 3,
        out_specs=pl.BlockSpec(memory_space=pl.ANY),
        scratch_shapes=[
            vmem((PAIRS, NY) + block, BF16),
            vmem((PAIRS, NY) + block, BF16),
            vmem((PAIRS, 2, NX) + block, BF16),
            vmem((PAIRS,) + block, BF16),
            vmem((512, 1024), BF16),
            vmem((256, 1024), BF16),
            vmem((PAIRS, NZ, TOK, 256), F32),
            vmem((PAIRS, 2, 4, TOK, 256), F32),
            vmem((PAIRS, 8, 8, LANES), F32),
            vmem((PAIRS, TOK, 256), F32),
            vmem((PAIRS, NZ, TOK, 256), BF16),
            vmem((PAIRS, 2, NX) + block, F32),
            vmem((PAIRS, NX) + block, F32),
            vmem((PAIRS, 3) + block, F32),
            vmem((PAIRS,) + block, BF16),
            vmem((PAIRS,) + block, BF16),
            dma((3, PAIRS)),
            dma((PAIRS,)),
            dma((PAIRS, 4, 2)), dma((PAIRS, 4, 2)),
            dma((PAIRS, 4, 2)), dma((PAIRS, 4, 2)),
            dma((PAIRS,)), dma((PAIRS,)),
            dma((PAIRS, 7)), dma((PAIRS, 7)),
            dma((PAIRS, 4, 2)), dma((PAIRS, 4, 2)),
            dma((PAIRS, 7)), dma((PAIRS, 7)),
            dma((PAIRS, 7)), dma((PAIRS, 7)),
            dma((PAIRS,)), dma((PAIRS,)),
            dma((PAIRS, 3)), dma((PAIRS, 3)),
            dma((PAIRS,)), dma((PAIRS,)),
        ],
        compiler_params=pltpu.CompilerParams(collective_id=0, has_side_effects=True, vmem_limit_bytes=40 << 20),
    )(queries, keys, values)


def solution(mesh):
    spec = P("seq", "res", None)
    return jax.shard_map(local, mesh=mesh, in_specs=(spec, spec, spec), out_specs=spec, check_vma=False)
```

```python
import functools

import jax
import jax.numpy as jnp
from jax import lax
from jax.experimental import pallas as pl
from jax.experimental.pallas import tpu as pltpu
from jax.sharding import PartitionSpec as P

NZ, NY, NX = 8, 8, 4
PAIRS = 3
ROWS, TOK, LANES = 4, 64, 128
EIGHT = TOK // NZ
HALF = NX * EIGHT
F32, BF16 = jnp.float32, jnp.bfloat16


def each(name, *arg):
    return [(name, p) + arg for p in range(PAIRS)]


ORDER = (
    each("q0") + each("k1") + each("q", 0) + each("k", 1) + each("q", 1) + each("k", 2) + each("q", 2) + each("k", 3)
    + each("v1") + each("build") + each("s") + each("z", 1) + each("z", 2) + each("v", 1) + each("z", 3) + each("v", 2)
    + each("local") + each("soft") + each("v", 3) + each("vcat")
)
for k in range(5):
    if k > 0:
        ORDER += each("p", k)
    ORDER += each("o", k) + each("sum", k)
    if k > 0:
        ORDER += each("mid", k - 1)
ORDER += each("mid", 4) + each("fin") + each("out")


def kernel(
    q_hbm, k_hbm, v_hbm, out_hbm,
    kbuf, vbuf, qbuf, qsend, qm, kcat, sbuf, zrecv, stat, statv, pbuf, vcat, obuf, orecv, xhalf, xfull, ofin, oown, oswap,
    load_sem, out_sem, k_ss, k_rs, v_ss, v_rs, qs_ss, qs_rs, qx_ss, qx_rs, qc_ss, qc_rs, z_ss, z_rs, st_ss, st_rs,
    p_ss, p_rs, o_ss, o_rs, xh_ss, xh_rs, xf_ss, xf_rs, w_ss, w_rs,
):
    s_id, r_id = lax.axis_index("seq"), lax.axis_index("res")
    z, yh = s_id // 2, s_id % 2
    yl, x, c = r_id // 8, (r_id // 2) % 4, r_id % 2
    y = yh * 4 + yl

    def at(z_=None, y_=None, x_=None, c_=None):
        z_ = z if z_ is None else z_
        y_ = y if y_ is None else y_
        x_ = x if x_ is None else x_
        c_ = c if c_ is None else c_
        return {"seq": z_ * 2 + y_ // 4, "res": ((y_ % 4) * 4 + x_) * 2 + c_}

    def zdev(k):
        return at(z_=(z + k + NZ) % NZ)

    def ydev(k):
        return at(y_=(y + k + NY) % NY)

    way_out = (yh + c) % 2
    taker = at(y_=(y + 2 - 4 * way_out + NY) % NY, c_=yh)
    way_in = ((y + 6) % NY // 4 + c) % 2
    owner = at(y_=(y - 2 + 4 * way_in + NY) % NY, c_=(c + way_in) % 2)
    sibling = at(c_=1 - c)

    def group(k):
        g = (x * 2 + c + k) % 8
        return at(x_=g // 2, c_=g % 2)

    def group_index(k):
        g = (x * 2 + c + k + 8) % 8
        return g // 2, g % 2

    def remote(src, dst, ss, rs, dev):
        return pltpu.make_async_remote_copy(
            src_ref=src, dst_ref=dst, send_sem=ss, recv_sem=rs, device_id=dev, device_id_type=pl.DeviceIdType.MESH
        )

    sent, due = [], {}

    def go(key, send, recv=None):
        send().start()
        sent.append(send)
        due[key] = recv or send

    def got(key):
        due.pop(key)().wait_recv()

    def lanes(p):
        return pl.ds(p * LANES, LANES)

    def load_k(p):
        return pltpu.make_async_copy(k_hbm.at[:, :, lanes(p)], kbuf.at[p, y], load_sem.at[0, p])

    def load_v(p):
        return pltpu.make_async_copy(v_hbm.at[:, :, lanes(p)], vbuf.at[p, y], load_sem.at[1, p])

    def load_q(p):
        return pltpu.make_async_copy(q_hbm.at[:, :, lanes(p)], qsend.at[p], load_sem.at[2, p])

    def ring(buf, ss, rs, p, step, way):
        src = (y - way * (step - 1) + NY) % NY
        half = pl.ds(0, ROWS) if step < 4 else (pl.ds(0, 2) if way == 1 else pl.ds(2, 2))
        d = 0 if way == 1 else 1
        view = buf.at[p, src, half]
        return remote(view, view, ss.at[p, step - 1, d], rs.at[p, step - 1, d], ydev(way))

    def ring_recv(buf, ss, rs, p, step, way):
        src = (y - way * step + NY) % NY
        half = pl.ds(0, ROWS) if step < 4 else (pl.ds(0, 2) if way == 1 else pl.ds(2, 2))
        d = 0 if way == 1 else 1
        view = buf.at[p, src, half]
        return remote(view, view, ss.at[p, step - 1, d], rs.at[p, step - 1, d], ydev(way))

    K = (kbuf, k_ss, k_rs)
    V = (vbuf, v_ss, v_rs)

    def ring_start(t, p, step):
        for way in (1, -1):
            go((t is K, p, step, way), functools.partial(ring, *t, p, step, way), functools.partial(ring_recv, *t, p, step, way))

    def ring_wait(t, p, step):
        for way in (1, -1):
            got((t is K, p, step, way))

    def q_move(p, slot, dev):
        return remote(qsend.at[p], qbuf.at[p, slot, x], qs_ss.at[p], qs_rs.at[p], dev)

    def q_start(p):
        load_q(p).wait()
        go(("qs", p), lambda: q_move(p, yh, taker), lambda: q_move(p, c, taker))

    def q_ring(p, step, way, behind):
        d = 0 if way == 1 else 1
        half = pl.ds(0, ROWS) if step == 1 else pl.ds(2 * d, 2)
        view = qbuf.at[p, c, (x - way * (step - 1 + behind) + NX) % NX, half]
        return remote(view, view, qx_ss.at[p, step - 1, d], qx_rs.at[p, step - 1, d], at(x_=(x + way + NX) % NX))

    def q_ring_start(p, step):
        for way in (1, -1):
            go(("qx", p, step, way), functools.partial(q_ring, p, step, way, 0), functools.partial(q_ring, p, step, way, 1))

    def q_step(p, step):
        if step == 0:
            got(("qs", p))
        else:
            for way in (1, -1):
                got(("qx", p, step, way))
        if step < 2:
            q_ring_start(p, step + 1)
        else:
            go(("qc", p), functools.partial(q_share, p), functools.partial(q_share_recv, p))

    def q_share(p):
        return remote(qbuf.at[p, c], qbuf.at[p, c], qc_ss.at[p], qc_rs.at[p], sibling)

    def q_share_recv(p):
        return remote(qbuf.at[p, 1 - c], qbuf.at[p, 1 - c], qc_ss.at[p], qc_rs.at[p], sibling)

    def q_spread_start(p, where):
        if where is at_home:
            at_home(lambda: load_q_home(p).wait())
        else:
            got(("qs", p))
        for k in (2, 1, 3):
            go(("qx", p, k, where), functools.partial(q_spread, p, k), functools.partial(q_spread_recv, p, k), where)

    lane = lax.broadcasted_iota(jnp.int32, (HALF, LANES), 1)

    def q_build(p):
        got(("qc", p))
        for g in range(2):
            for r in range(ROWS):
                cols = pl.ds((g * ROWS + r) * LANES, LANES)
                block = qbuf[p, g, :, r].astype(F32)
                for s in range(NZ):
                    part = jnp.concatenate([block[i, s * EIGHT : (s + 1) * EIGHT] for i in range(NX)], axis=0)
                    zero = jnp.zeros_like(part)
                    qm[p, s, 0, :, cols] = jnp.where(lane < 64, part, zero).astype(BF16)
                    qm[p, s, 1, :, cols] = jnp.where(lane >= 64, part, zero).astype(BF16)

    def scores(p):
        ring_wait(K, p, 4)
        for g in range(2):
            for r in range(ROWS):
                cols = pl.ds((g * ROWS + r) * LANES, LANES)
                kcat[:, cols] = kbuf[p, g * 4 : g * 4 + 4, r].reshape(256, LANES)
        for half in range(2):
            part = lax.dot_general(
                qm[p, half * 4 : half * 4 + 4].reshape(256, 1024), kcat[...], (((1,), (1,)), ((), ())), preferred_element_type=F32
            )
            sbuf[p, half * 4 : half * 4 + 4] = part.reshape(4, TOK, 256)
        z_start(p, 1)

    def zslice(way, step):
        return (z + way * (5 - step) + NZ) % NZ

    def z_copy(p, step, way):
        d = 0 if way == 1 else 1
        half = pl.ds(0, TOK) if step > 1 else pl.ds(d * 32, 32)
        return remote(
            sbuf.at[p, zslice(way, step), half],
            zrecv.at[p, d, step - 1, half],
            z_ss.at[p, step - 1, d],
            z_rs.at[p, step - 1, d],
            zdev(way),
        )

    def z_start(p, step):
        for way in (1, -1):
            go(("z", p, step, way), functools.partial(z_copy, p, step, way))

    def z_add(p, step):
        for way in (1, -1):
            d = 0 if way == 1 else 1
            got(("z", p, step, way))
            s = zslice(way, step + 1)
            if step == 1:
                rows = pl.ds(d * 32, 32)
                sbuf[p, s, rows] = sbuf[p, s, rows] + zrecv[p, d, 0, rows]
            else:
                sbuf[p, s] = sbuf[p, s] + zrecv[p, d, step - 1]
        z_start(p, step + 1)

    def stat_copy(p, k):
        return remote(stat.at[p, 0], stat.at[p, k], st_ss.at[p, k - 1], st_rs.at[p, k - 1], group(k))

    def softmax_local(p):
        for way in (1, -1):
            got(("z", p, 4, way))
        s = sbuf[p, z] + zrecv[p, 0, 3] + zrecv[p, 1, 3]
        s = s * (1.0 / 64.0)
        m = jnp.max(s, axis=1, keepdims=True)
        e = jnp.exp(s - m)
        l = jnp.sum(e, axis=1, keepdims=True)
        statv[p] = e
        col = lax.broadcasted_iota(jnp.int32, (TOK, LANES), 1)
        both = jnp.where(col == 0, m, l)
        tall = jnp.concatenate([both, both], axis=0)
        stat[p, 0] = jnp.transpose(tall)[0:8, :]
        for k in range(1, 8):
            go(("st", p, k), functools.partial(stat_copy, p, k))

    def softmax_global(p):
        for k in range(1, 8):
            got(("st", p, k))
        m = stat[p, 0, 0:1, :]
        for k in range(1, 8):
            m = jnp.maximum(m, stat[p, k, 0:1, :])
        l = jnp.zeros_like(m)
        for k in range(8):
            l = l + jnp.exp(stat[p, k, 0:1, :] - m) * stat[p, k, 1:2, :]
        factor = jnp.exp(stat[p, 0, 0:1, :] - m) / l
        tall = jnp.transpose(jnp.broadcast_to(factor, (LANES, LANES)))
        pbuf[p, z] = (statv[p] * tall[0:TOK, 0:1]).astype(BF16)
        p_start(p, 1)

    def p_view(p, step, way, slot):
        half = pl.ds(0, TOK) if step < 4 else pl.ds(0 if way == 1 else 32, 32)
        return pbuf.at[p, (slot + 2 * NZ) % NZ, half]

    def p_copy(p, step, way, behind):
        d = 0 if way == 1 else 1
        view = p_view(p, step, way, z - way * (step - 1 + behind))
        return remote(view, view, p_ss.at[p, step - 1, d], p_rs.at[p, step - 1, d], zdev(way))

    def p_start(p, step):
        for way in (1, -1):
            go(("p", p, step, way), functools.partial(p_copy, p, step, way, 0), functools.partial(p_copy, p, step, way, 1))

    def p_wait(p, step):
        for way in (1, -1):
            got(("p", p, step, way))

    def v_build(p):
        ring_wait(V, p, 4)
        for g in range(2):
            for r in range(ROWS):
                vcat[p, g, :, pl.ds(r * LANES, LANES)] = vbuf[p, g * 4 : g * 4 + 4, r].reshape(256, LANES)

    first = lax.broadcasted_iota(jnp.int32, (HALF, ROWS * LANES), 1) % LANES < 64

    def slices(k):
        if k == 0:
            return [z]
        if k == 4:
            return [(z + 4) % NZ]
        return [(z + NZ - k) % NZ, (z + k) % NZ]

    def line(k):
        return pl.ds(0, 1) if k == 0 else pl.ds(2 * k - 1, 1 if k == 4 else 2)

    def places(k):
        return range(line(k).start, line(k).start + line(k).size)

    def o_copy(p, k):
        return remote(obuf.at[p, 1 - c, line(k)], orecv.at[p, line(k)], o_ss.at[p, k], o_rs.at[p, k], sibling)

    def x_half(p, k, way):
        d = 0 if way == 1 else 1
        return remote(
            obuf.at[p, c, line(k), (x + 2) % NX, :, pl.ds(256 * d, 256)], xhalf.at[p, d, line(k)],
            xh_ss.at[p, k, d], xh_rs.at[p, k, d], at(x_=(x + way + NX) % NX),
        )

    def x_full(p, k, way):
        d = 0 if way == 1 else 1
        to = (x + way + NX) % NX
        return remote(obuf.at[p, c, line(k), to], xfull.at[p, d, line(k)], xf_ss.at[p, k, d], xf_rs.at[p, k, d], at(x_=to))

    def attend(p, k):
        parts = slices(k)
        probs = [pbuf[p, s] for s in parts]
        probs = probs[0] if len(probs) == 1 else jnp.concatenate(probs, axis=0)
        for g in (1 - c, c):
            o = lax.dot_general(probs, vcat[p, g], (((1,), (0,)), ((), ())), preferred_element_type=F32)
            for t in range(len(parts)):
                both = jnp.where(first, o[t * TOK : t * TOK + HALF], o[t * TOK + HALF : (t + 1) * TOK])
                obuf[p, g, line(k).start + t] = both.reshape(NX, EIGHT, ROWS * LANES)
            if g is not c:
                go(("o", p, k), functools.partial(o_copy, p, k))

    def chip_sum(p, k):
        got(("o", p, k))
        for n in places(k):
            obuf[p, c, n] = obuf[p, c, n] + orecv[p, n]
        for way in (1, -1):
            go(("xh", p, k, way), functools.partial(x_half, p, k, way))

    def x_sum(p, k):
        for way in (1, -1):
            d = 0 if way == 1 else 1
            got(("xh", p, k, way))
            to = (x + way + NX) % NX
            cols = pl.ds(256 * d, 256)
            for n in places(k):
                obuf[p, c, n, to, :, cols] = obuf[p, c, n, to, :, cols] + xhalf[p, d, n]
            go(("xf", p, k, way), functools.partial(x_full, p, k, way))

    def out_copy(p):
        return pltpu.make_async_copy(oswap.at[p], out_hbm.at[:, :, lanes(p)], out_sem.at[p])

    def w_copy(p):
        return remote(oown.at[p], oswap.at[p], w_ss.at[p], w_rs.at[p], owner)

    def finish(p):
        for k in range(5):
            for way in (1, -1):
                got(("xf", p, k, way))
            for t, s in enumerate(slices(k)):
                n = line(k).start + t
                ofin[p, s] = obuf[p, c, n, x] + xfull[p, 0, n] + xfull[p, 1, n]
        for r in range(ROWS):
            oown[p, r] = ofin[p, :, :, r * LANES : (r + 1) * LANES].reshape(TOK, LANES).astype(BF16)
        go(("w", p), functools.partial(w_copy, p))

    def leave(p):
        got(("w", p))
        out_copy(p).start()

    pairs = range(PAIRS)
    for p in pairs:
        load_q(p).start()
        load_k(p).start()
    for p in pairs:
        load_v(p).start()

    barrier = pltpu.get_barrier_semaphore()
    peers = [zdev(1), zdev(-1), ydev(1), ydev(-1), taker, owner] + [group(k) for k in range(1, 8)]
    for dev in peers:
        pl.semaphore_signal(barrier, inc=1, device_id=dev, device_id_type=pl.DeviceIdType.MESH)
    pl.semaphore_wait(barrier, len(peers))

    def schedule():
        def k_step(p, step):
            ring_wait(K, p, step)
            ring_start(K, p, step + 1)

        def v_step(p, step):
            ring_wait(V, p, step)
            ring_start(V, p, step + 1)

        def k_first(p):
            load_k(p).wait()
            ring_start(K, p, 1)

        def v_first(p):
            load_v(p).wait()
            ring_start(V, p, 1)

        def p_step(p, k):
            p_wait(p, k)
            if k < 4:
                p_start(p, k + 1)

        act = dict(
            q0=q_start, q=q_step, build=q_build, k1=k_first, k=k_step, s=scores, z=z_add, local=softmax_local,
            soft=softmax_global, v1=v_first, v=v_step, vcat=v_build, p=p_step, o=attend, sum=chip_sum, mid=x_sum,
            fin=finish, out=leave,
        )
        for name, *arg in ORDER:
            act[name](*arg)

    schedule()

    for copy in due.values():
        copy().wait_recv()
    for copy in sent:
        copy().wait_send()
    for p in pairs:
        out_copy(p).wait()


def local(queries, keys, values):
    vmem = pltpu.VMEM
    dma = pltpu.SemaphoreType.DMA
    block = (ROWS, TOK, LANES)
    return pl.pallas_call(
        kernel,
        out_shape=jax.ShapeDtypeStruct(queries.shape, BF16),
        in_specs=[pl.BlockSpec(memory_space=pl.ANY)] * 3,
        out_specs=pl.BlockSpec(memory_space=pl.ANY),
        scratch_shapes=[
            vmem((PAIRS, NY) + block, BF16),
            vmem((PAIRS, NY) + block, BF16),
            vmem((PAIRS, 2, NX) + block, BF16),
            vmem((PAIRS,) + block, BF16),
            vmem((PAIRS, NZ, 2, HALF, 1024), BF16),
            vmem((256, 1024), BF16),
            vmem((PAIRS, NZ, TOK, 256), F32),
            vmem((PAIRS, 2, 4, TOK, 256), F32),
            vmem((PAIRS, 8, 8, LANES), F32),
            vmem((PAIRS, TOK, 256), F32),
            vmem((PAIRS, NZ, TOK, 256), BF16),
            vmem((PAIRS, 2, 256, 512), BF16),
            vmem((PAIRS, 2, NZ, NX, EIGHT, 512), F32),
            vmem((PAIRS, NZ, NX, EIGHT, 512), F32),
            vmem((PAIRS, 2, NZ, EIGHT, 256), F32),
            vmem((PAIRS, 2, NZ, EIGHT, 512), F32),
            vmem((PAIRS, NZ, EIGHT, 512), F32),
            vmem((PAIRS,) + block, BF16),
            vmem((PAIRS,) + block, BF16),
            dma((3, PAIRS)),
            dma((PAIRS,)),
            dma((PAIRS, 4, 2)), dma((PAIRS, 4, 2)),
            dma((PAIRS, 4, 2)), dma((PAIRS, 4, 2)),
            dma((PAIRS,)), dma((PAIRS,)),
            dma((PAIRS, 2, 2)), dma((PAIRS, 2, 2)),
            dma((PAIRS,)), dma((PAIRS,)),
            dma((PAIRS, 4, 2)), dma((PAIRS, 4, 2)),
            dma((PAIRS, 7)), dma((PAIRS, 7)),
            dma((PAIRS, 4, 2)), dma((PAIRS, 4, 2)),
            dma((PAIRS, 5)), dma((PAIRS, 5)),
            dma((PAIRS, 5, 2)), dma((PAIRS, 5, 2)),
            dma((PAIRS, 5, 2)), dma((PAIRS, 5, 2)),
            dma((PAIRS,)), dma((PAIRS,)),
        ],
        compiler_params=pltpu.CompilerParams(collective_id=0, has_side_effects=True, vmem_limit_bytes=63 << 20),
    )(queries, keys, values)


def solution(mesh):
    spec = P("seq", "res", None)
    return jax.shard_map(local, mesh=mesh, in_specs=(spec, spec, spec), out_specs=spec, check_vma=False)
```

```python
import functools

import jax
import jax.numpy as jnp
from jax import lax
from jax.experimental import pallas as pl
from jax.experimental.pallas import tpu as pltpu
from jax.sharding import PartitionSpec as P

NZ, NY, NX = 8, 8, 4
PAIRS = 3
ROWS, TOK, LANES = 4, 64, 128
EIGHT = TOK // NZ
HALF = NX * EIGHT
F32, BF16 = jnp.float32, jnp.bfloat16


ORDER = [
    ("q0", 0), ("q0", 1), ("q0", 2), ("qw", 0), ("qw", 1), ("qw", 2), ("k1", 0), ("k1", 1), ("k1", 2), ("q", 0, 0),
    ("q", 1, 0), ("q", 2, 0), ("k", 0, 1), ("k", 1, 1), ("k", 2, 1), ("q", 0, 1), ("q", 1, 1), ("q", 2, 1),
    ("k", 0, 2), ("k", 1, 2), ("k", 2, 2), ("q", 0, 2), ("q", 1, 2), ("q", 2, 2), ("k", 0, 3), ("k", 1, 3),
    ("k", 2, 3), ("v1", 0), ("v1", 1), ("v1", 2), ("build", 0), ("build", 1), ("build", 2), ("s", 0), ("s", 1),
    ("s", 2), ("z", 0, 1), ("z", 1, 1), ("z", 2, 1), ("v", 0, 1), ("v", 1, 1), ("v", 2, 1), ("z", 0, 2), ("z", 1, 2),
    ("z", 2, 2), ("v", 0, 2), ("v", 1, 2), ("v", 2, 2), ("z", 0, 3), ("z", 1, 3), ("z", 2, 3), ("v", 0, 3),
    ("v", 1, 3), ("v", 2, 3), ("local", 0), ("local", 1), ("local", 2), ("soft", 0), ("soft", 1), ("soft", 2),
    ("vcat", 0), ("vcat", 1), ("vcat", 2), ("o", 0, 0), ("o", 1, 0), ("o", 2, 0), ("sum", 0, 0), ("sum", 1, 0),
    ("sum", 2, 0), ("p", 0, 1), ("p", 1, 1), ("p", 2, 1), ("o", 0, 1), ("o", 1, 1), ("o", 2, 1), ("sum", 0, 1),
    ("sum", 1, 1), ("sum", 2, 1), ("mid", 0, 0), ("mid", 1, 0), ("mid", 2, 0), ("p", 0, 2), ("p", 1, 2), ("p", 2, 2),
    ("o", 0, 2), ("o", 1, 2), ("o", 2, 2), ("sum", 0, 2), ("sum", 1, 2), ("sum", 2, 2), ("mid", 0, 1), ("mid", 1, 1),
    ("mid", 2, 1), ("p", 0, 3), ("p", 1, 3), ("p", 2, 3), ("o", 0, 3), ("o", 1, 3), ("o", 2, 3), ("sum", 0, 3),
    ("sum", 1, 3), ("sum", 2, 3), ("mid", 0, 2), ("mid", 1, 2), ("mid", 2, 2), ("p", 0, 4), ("o", 0, 4),
    ("sum", 0, 4), ("p", 1, 4), ("o", 1, 4), ("sum", 1, 4), ("p", 2, 4), ("o", 2, 4), ("sum", 2, 4), ("mid", 0, 3),
    ("mid", 1, 3), ("mid", 2, 3), ("fin", 0), ("fin", 1), ("fin", 2),
]


def kernel(
    q_hbm, k_hbm, v_hbm, out_hbm,
    kbuf, vbuf, qbuf, qsend, qm, kcat, sbuf, zrecv, stat, statv, pbuf, vcat, obuf, orecv, xhalf, xfull, ofin, oown,
    load_sem, k_ss, k_rs, v_ss, v_rs, qs_ss, qs_rs, qx_ss, qx_rs, qc_ss, qc_rs, z_ss, z_rs, st_ss, st_rs,
    p_ss, p_rs, o_ss, o_rs, xh_ss, xh_rs, xf_ss, xf_rs, w_ss, w_rs,
):
    s_id, r_id = lax.axis_index("seq"), lax.axis_index("res")
    z, yh = s_id // 2, s_id % 2
    yl, x, c = r_id // 8, (r_id // 2) % 4, r_id % 2
    y = yh * 4 + yl

    def at(z_=None, y_=None, x_=None, c_=None):
        z_ = z if z_ is None else z_
        y_ = y if y_ is None else y_
        x_ = x if x_ is None else x_
        c_ = c if c_ is None else c_
        return {"seq": z_ * 2 + y_ // 4, "res": ((y_ % 4) * 4 + x_) * 2 + c_}

    def zdev(k):
        return at(z_=(z + k + NZ) % NZ)

    def ydev(k):
        return at(y_=(y + k + NY) % NY)

    way_out = (yh + c) % 2
    taker = at(y_=(y + 2 - 4 * way_out + NY) % NY, c_=yh)
    way_in = ((y + 6) % NY // 4 + c) % 2
    owner = at(y_=(y - 2 + 4 * way_in + NY) % NY, c_=(c + way_in) % 2)
    sibling = at(c_=1 - c)

    def group(k):
        g = (x * 2 + c + k) % 8
        return at(x_=g // 2, c_=g % 2)

    def group_index(k):
        g = (x * 2 + c + k + 8) % 8
        return g // 2, g % 2

    def remote(src, dst, ss, rs, dev):
        return pltpu.make_async_remote_copy(
            src_ref=src, dst_ref=dst, send_sem=ss, recv_sem=rs, device_id=dev, device_id_type=pl.DeviceIdType.MESH
        )

    sent, due = {}, {}

    def go(key, send, recv=None):
        send().start()
        sent[key] = send
        due[key] = recv or send

    def got(key):
        due.pop(key)().wait_recv()

    def left(*keys):
        for key in keys:
            sent.pop(key)().wait_send()

    def lanes(p):
        return pl.ds(p * LANES, LANES)

    def load_k(p):
        return pltpu.make_async_copy(k_hbm.at[:, :, lanes(p)], kbuf.at[p, y], load_sem.at[0, p])

    def load_v(p):
        return pltpu.make_async_copy(v_hbm.at[:, :, lanes(p)], vbuf.at[p, y], load_sem.at[1, p])

    def load_q(p):
        return pltpu.make_async_copy(q_hbm.at[:, :, lanes(p)], qsend.at[p], load_sem.at[2, p])

    def ring(buf, ss, rs, p, step, way):
        src = (y - way * (step - 1) + NY) % NY
        half = pl.ds(0, ROWS) if step < 4 else (pl.ds(0, 2) if way == 1 else pl.ds(2, 2))
        d = 0 if way == 1 else 1
        view = buf.at[p, src, half]
        return remote(view, view, ss.at[p, step - 1, d], rs.at[p, step - 1, d], ydev(way))

    def ring_recv(buf, ss, rs, p, step, way):
        src = (y - way * step + NY) % NY
        half = pl.ds(0, ROWS) if step < 4 else (pl.ds(0, 2) if way == 1 else pl.ds(2, 2))
        d = 0 if way == 1 else 1
        view = buf.at[p, src, half]
        return remote(view, view, ss.at[p, step - 1, d], rs.at[p, step - 1, d], ydev(way))

    K = (kbuf, k_ss, k_rs)
    V = (vbuf, v_ss, v_rs)

    def ring_start(t, p, step):
        for way in (1, -1):
            go((t is K, p, step, way), functools.partial(ring, *t, p, step, way), functools.partial(ring_recv, *t, p, step, way))

    def ring_wait(t, p, step):
        for way in (1, -1):
            got((t is K, p, step, way))

    def q_move(p, slot, dev):
        return remote(qsend.at[p], qbuf.at[p, slot, x], qs_ss.at[p], qs_rs.at[p], dev)

    def q_start(p):
        load_q(p).wait()
        go(("qs", p), lambda: q_move(p, yh, taker), lambda: q_move(p, c, taker))

    def q_ring(p, step, way, behind):
        d = 0 if way == 1 else 1
        half = pl.ds(0, ROWS) if step == 1 else pl.ds(2 * d, 2)
        view = qbuf.at[p, c, (x - way * (step - 1 + behind) + NX) % NX, half]
        return remote(view, view, qx_ss.at[p, step - 1, d], qx_rs.at[p, step - 1, d], at(x_=(x + way + NX) % NX))

    def q_ring_start(p, step):
        for way in (1, -1):
            go(("qx", p, step, way), functools.partial(q_ring, p, step, way, 0), functools.partial(q_ring, p, step, way, 1))

    def q_step(p, step):
        if step == 0:
            got(("qs", p))
        else:
            for way in (1, -1):
                got(("qx", p, step, way))
        if step < 2:
            q_ring_start(p, step + 1)
        else:
            go(("qc", p), functools.partial(q_share, p), functools.partial(q_share_recv, p))

    def q_share(p):
        return remote(qbuf.at[p, c], qbuf.at[p, c], qc_ss.at[p], qc_rs.at[p], sibling)

    def q_share_recv(p):
        return remote(qbuf.at[p, 1 - c], qbuf.at[p, 1 - c], qc_ss.at[p], qc_rs.at[p], sibling)

    def q_spread_start(p, where):
        if where is at_home:
            at_home(lambda: load_q_home(p).wait())
        else:
            got(("qs", p))
        for k in (2, 1, 3):
            go(("qx", p, k, where), functools.partial(q_spread, p, k), functools.partial(q_spread_recv, p, k), where)

    lane = lax.broadcasted_iota(jnp.int32, (HALF, LANES), 1)

    def q_build(p):
        got(("qc", p))
        for g in range(2):
            for r in range(ROWS):
                cols = pl.ds((g * ROWS + r) * LANES, LANES)
                block = qbuf[p, g, :, r].astype(F32)
                for s in range(NZ):
                    part = jnp.concatenate([block[i, s * EIGHT : (s + 1) * EIGHT] for i in range(NX)], axis=0)
                    zero = jnp.zeros_like(part)
                    qm[p, s, 0, :, cols] = jnp.where(lane < 64, part, zero).astype(BF16)
                    qm[p, s, 1, :, cols] = jnp.where(lane >= 64, part, zero).astype(BF16)

    def scores(p):
        ring_wait(K, p, 4)
        for g in range(2):
            for r in range(ROWS):
                cols = pl.ds((g * ROWS + r) * LANES, LANES)
                kcat[:, cols] = kbuf[p, g * 4 : g * 4 + 4, r].reshape(256, LANES)
        for half in range(2):
            part = lax.dot_general(
                qm[p, half * 4 : half * 4 + 4].reshape(256, 1024), kcat[...], (((1,), (1,)), ((), ())), preferred_element_type=F32
            )
            sbuf[p, half * 4 : half * 4 + 4] = part.reshape(4, TOK, 256)
        z_start(p, 1)

    def zslice(way, step):
        return (z + way * (5 - step) + NZ) % NZ

    def z_copy(p, step, way):
        d = 0 if way == 1 else 1
        half = pl.ds(0, TOK) if step > 1 else pl.ds(d * 32, 32)
        return remote(
            sbuf.at[p, zslice(way, step), half],
            zrecv.at[p, d, step - 1, half],
            z_ss.at[p, step - 1, d],
            z_rs.at[p, step - 1, d],
            zdev(way),
        )

    def z_start(p, step):
        for way in (1, -1):
            go(("z", p, step, way), functools.partial(z_copy, p, step, way))

    def z_add(p, step):
        for way in (1, -1):
            d = 0 if way == 1 else 1
            got(("z", p, step, way))
            s = zslice(way, step + 1)
            if step == 1:
                rows = pl.ds(d * 32, 32)
                sbuf[p, s, rows] = sbuf[p, s, rows] + zrecv[p, d, 0, rows]
            else:
                sbuf[p, s] = sbuf[p, s] + zrecv[p, d, step - 1]
        z_start(p, step + 1)

    def stat_copy(p, k):
        return remote(stat.at[p, 0], stat.at[p, k], st_ss.at[p, k - 1], st_rs.at[p, k - 1], group(k))

    def softmax_local(p):
        for way in (1, -1):
            got(("z", p, 4, way))
        s = sbuf[p, z] + zrecv[p, 0, 3] + zrecv[p, 1, 3]
        s = s * (1.0 / 64.0)
        m = jnp.max(s, axis=1, keepdims=True)
        e = jnp.exp(s - m)
        l = jnp.sum(e, axis=1, keepdims=True)
        statv[p] = e
        col = lax.broadcasted_iota(jnp.int32, (TOK, LANES), 1)
        both = jnp.where(col == 0, m, l)
        tall = jnp.concatenate([both, both], axis=0)
        stat[p, 0] = jnp.transpose(tall)[0:8, :]
        for k in range(1, 8):
            go(("st", p, k), functools.partial(stat_copy, p, k))

    def softmax_global(p):
        for k in range(1, 8):
            got(("st", p, k))
        m = stat[p, 0, 0:1, :]
        for k in range(1, 8):
            m = jnp.maximum(m, stat[p, k, 0:1, :])
        l = jnp.zeros_like(m)
        for k in range(8):
            l = l + jnp.exp(stat[p, k, 0:1, :] - m) * stat[p, k, 1:2, :]
        factor = jnp.exp(stat[p, 0, 0:1, :] - m) / l
        tall = jnp.transpose(jnp.broadcast_to(factor, (LANES, LANES)))
        pbuf[p, z] = (statv[p] * tall[0:TOK, 0:1]).astype(BF16)
        p_start(p, 1)

    def p_view(p, step, way, slot):
        half = pl.ds(0, TOK) if step < 4 else pl.ds(0 if way == 1 else 32, 32)
        return pbuf.at[p, (slot + 2 * NZ) % NZ, half]

    def p_copy(p, step, way, behind):
        d = 0 if way == 1 else 1
        view = p_view(p, step, way, z - way * (step - 1 + behind))
        return remote(view, view, p_ss.at[p, step - 1, d], p_rs.at[p, step - 1, d], zdev(way))

    def p_start(p, step):
        for way in (1, -1):
            go(("p", p, step, way), functools.partial(p_copy, p, step, way, 0), functools.partial(p_copy, p, step, way, 1))

    def p_wait(p, step):
        for way in (1, -1):
            got(("p", p, step, way))

    def v_build(p):
        ring_wait(V, p, 4)
        for g in range(2):
            for r in range(ROWS):
                vcat[p, g, :, pl.ds(r * LANES, LANES)] = vbuf[p, g * 4 : g * 4 + 4, r].reshape(256, LANES)

    first = lax.broadcasted_iota(jnp.int32, (HALF, ROWS * LANES), 1) % LANES < 64

    def slices(k):
        if k == 0:
            return [z]
        if k == 4:
            return [(z + 4) % NZ]
        return [(z + NZ - k) % NZ, (z + k) % NZ]

    def line(k):
        return pl.ds(0, 1) if k == 0 else pl.ds(2 * k - 1, 1 if k == 4 else 2)

    def places(k):
        return range(line(k).start, line(k).start + line(k).size)

    def o_copy(p, k):
        return remote(obuf.at[p, 1 - c, line(k)], orecv.at[p, line(k)], o_ss.at[p, k], o_rs.at[p, k], sibling)

    def x_half(p, k, way):
        d = 0 if way == 1 else 1
        return remote(
            obuf.at[p, c, line(k), (x + 2) % NX, :, pl.ds(256 * d, 256)], xhalf.at[p, d, line(k)],
            xh_ss.at[p, k, d], xh_rs.at[p, k, d], at(x_=(x + way + NX) % NX),
        )

    def x_full(p, k, way):
        d = (1, -1, 2).index(way)
        to = (x + way + NX) % NX
        return remote(obuf.at[p, c, line(k), to], xfull.at[p, d, line(k)], xf_ss.at[p, k, d], xf_rs.at[p, k, d], at(x_=to))

    def attend(p, k):
        parts = slices(k)
        probs = [pbuf[p, s] for s in parts]
        probs = probs[0] if len(probs) == 1 else jnp.concatenate(probs, axis=0)
        for g in (1 - c, c):
            o = lax.dot_general(probs, vcat[p, g], (((1,), (0,)), ((), ())), preferred_element_type=F32)
            for t in range(len(parts)):
                both = jnp.where(first, o[t * TOK : t * TOK + HALF], o[t * TOK + HALF : (t + 1) * TOK])
                obuf[p, g, line(k).start + t] = both.reshape(NX, EIGHT, ROWS * LANES)
            if g is not c:
                go(("o", p, k), functools.partial(o_copy, p, k))

    def chip_sum(p, k):
        got(("o", p, k))
        for n in places(k):
            obuf[p, c, n] = obuf[p, c, n] + orecv[p, n]
        if k == 4:
            for way in (2, 1, -1):
                go(("xf", p, k, way), functools.partial(x_full, p, k, way))
            return
        for way in (1, -1):
            go(("xh", p, k, way), functools.partial(x_half, p, k, way))

    def x_sum(p, k):
        for way in (1, -1):
            d = 0 if way == 1 else 1
            got(("xh", p, k, way))
            to = (x + way + NX) % NX
            cols = pl.ds(256 * d, 256)
            for n in places(k):
                obuf[p, c, n, to, :, cols] = obuf[p, c, n, to, :, cols] + xhalf[p, d, n]
            go(("xf", p, k, way), functools.partial(x_full, p, k, way))

    def w_copy(p):
        return remote(oown.at[p], out_hbm.at[:, :, lanes(p)], w_ss.at[p], w_rs.at[p], owner)

    def finish(p):
        for k in range(5):
            for way in (1, -1) if k < 4 else (1, -1, 2):
                got(("xf", p, k, way))
            for t, s in enumerate(slices(k)):
                n = line(k).start + t
                total = obuf[p, c, n, x] + xfull[p, 0, n] + xfull[p, 1, n]
                ofin[p, s] = total if k < 4 else total + xfull[p, 2, n]
        for r in range(ROWS):
            oown[p, r] = ofin[p, :, :, r * LANES : (r + 1) * LANES].reshape(TOK, LANES).astype(BF16)
        go(("w", p), functools.partial(w_copy, p))

    pairs = range(PAIRS)
    for p in pairs:
        load_q(p).start()
        load_k(p).start()
    for p in pairs:
        load_v(p).start()

    barrier = pltpu.get_barrier_semaphore()
    peers = [zdev(1), zdev(-1), ydev(1), ydev(-1), taker, owner] + [group(k) for k in range(1, 8)]
    for dev in peers:
        pl.semaphore_signal(barrier, inc=1, device_id=dev, device_id_type=pl.DeviceIdType.MESH)
    pl.semaphore_wait(barrier, len(peers))

    def schedule():
        def k_step(p, step):
            ring_wait(K, p, step)
            ring_start(K, p, step + 1)

        def v_step(p, step):
            ring_wait(V, p, step)
            ring_start(V, p, step + 1)

        def k_first(p):
            load_k(p).wait()
            ring_start(K, p, 1)

        def v_first(p):
            load_v(p).wait()
            ring_start(V, p, 1)

        def p_step(p, k):
            p_wait(p, k)
            if k < 4:
                p_start(p, k + 1)

        act = dict(
            q0=q_start, q=q_step, build=q_build, k1=k_first, k=k_step, s=scores, z=z_add, local=softmax_local,
            soft=softmax_global, v1=v_first, v=v_step, vcat=v_build, p=p_step, o=attend, sum=chip_sum, mid=x_sum,
            fin=finish, qw=lambda p: left(("qs", p)), kw=lambda p: left((True, p, 1, 1), (True, p, 1, -1)),
            pw=lambda p: left(("p", p, 1, 1), ("p", p, 1, -1)),
        )
        for name, *arg in ORDER:
            act[name](*arg)

    schedule()

    for copy in due.values():
        copy().wait_recv()
    for copy in sent.values():
        copy().wait_send()


def local(queries, keys, values):
    vmem = pltpu.VMEM
    dma = pltpu.SemaphoreType.DMA
    block = (ROWS, TOK, LANES)
    return pl.pallas_call(
        kernel,
        out_shape=jax.ShapeDtypeStruct(queries.shape, BF16),
        in_specs=[pl.BlockSpec(memory_space=pl.ANY)] * 3,
        out_specs=pl.BlockSpec(memory_space=pl.ANY),
        scratch_shapes=[
            vmem((PAIRS, NY) + block, BF16),
            vmem((PAIRS, NY) + block, BF16),
            vmem((PAIRS, 2, NX) + block, BF16),
            vmem((PAIRS,) + block, BF16),
            vmem((PAIRS, NZ, 2, HALF, 1024), BF16),
            vmem((256, 1024), BF16),
            vmem((PAIRS, NZ, TOK, 256), F32),
            vmem((PAIRS, 2, 4, TOK, 256), F32),
            vmem((PAIRS, 8, 8, LANES), F32),
            vmem((PAIRS, TOK, 256), F32),
            vmem((PAIRS, NZ, TOK, 256), BF16),
            vmem((PAIRS, 2, 256, 512), BF16),
            vmem((PAIRS, 2, NZ, NX, EIGHT, 512), F32),
            vmem((PAIRS, NZ, NX, EIGHT, 512), F32),
            vmem((PAIRS, 2, NZ, EIGHT, 256), F32),
            vmem((PAIRS, 3, NZ, EIGHT, 512), F32),
            vmem((PAIRS, NZ, EIGHT, 512), F32),
            vmem((PAIRS,) + block, BF16),
            dma((3, PAIRS)),
            dma((PAIRS, 4, 2)), dma((PAIRS, 4, 2)),
            dma((PAIRS, 4, 2)), dma((PAIRS, 4, 2)),
            dma((PAIRS,)), dma((PAIRS,)),
            dma((PAIRS, 2, 2)), dma((PAIRS, 2, 2)),
            dma((PAIRS,)), dma((PAIRS,)),
            dma((PAIRS, 4, 2)), dma((PAIRS, 4, 2)),
            dma((PAIRS, 7)), dma((PAIRS, 7)),
            dma((PAIRS, 4, 2)), dma((PAIRS, 4, 2)),
            dma((PAIRS, 5)), dma((PAIRS, 5)),
            dma((PAIRS, 5, 2)), dma((PAIRS, 5, 2)),
            dma((PAIRS, 5, 3)), dma((PAIRS, 5, 3)),
            dma((PAIRS,)), dma((PAIRS,)),
        ],
        compiler_params=pltpu.CompilerParams(collective_id=0, has_side_effects=True, vmem_limit_bytes=63 << 20),
    )(queries, keys, values)


def solution(mesh):
    spec = P("seq", "res", None)
    return jax.shard_map(local, mesh=mesh, in_specs=(spec, spec, spec), out_specs=spec, check_vma=False)
```

```python
import functools

import jax
import jax.numpy as jnp
from jax import lax
from jax.experimental import pallas as pl
from jax.experimental.pallas import tpu as pltpu
from jax.sharding import PartitionSpec as P

NZ, NY, NX = 8, 8, 4
PAIRS = 3
ROWS, TOK, LANES = 4, 64, 128
EIGHT = TOK // NZ
HALF = NX * EIGHT
F32, BF16 = jnp.float32, jnp.bfloat16


ORDER = [
    ("q0", 0), ("q0", 1), ("q0", 2), ("qw", 0), ("qw", 1), ("qw", 2), ("k1", 0), ("k1", 1), ("k1", 2), ("vl", 0),
    ("vl", 1), ("vl", 2), ("q", 0, 0), ("q", 1, 0), ("q", 2, 0), ("k", 0, 1), ("k", 1, 1), ("k", 2, 1), ("q", 0, 1),
    ("q", 1, 1), ("q", 2, 1), ("k", 0, 2), ("k", 1, 2), ("k", 2, 2), ("q", 0, 2), ("q", 1, 2), ("q", 2, 2),
    ("k", 0, 3), ("k", 1, 3), ("k", 2, 3), ("v1", 0), ("v1", 1), ("v1", 2), ("build", 0), ("build", 1), ("build", 2),
    ("s", 0), ("s", 1), ("s", 2), ("z", 0, 1), ("z", 1, 1), ("z", 2, 1), ("v", 0, 1), ("v", 1, 1), ("v", 2, 1),
    ("z", 0, 2), ("z", 1, 2), ("z", 2, 2), ("v", 0, 2), ("v", 1, 2), ("v", 2, 2), ("z", 0, 3), ("z", 1, 3),
    ("z", 2, 3), ("v", 0, 3), ("v", 1, 3), ("v", 2, 3), ("local", 0), ("local", 1), ("local", 2), ("soft", 0),
    ("soft", 1), ("soft", 2), ("vcat", 0), ("vcat", 1), ("vcat", 2), ("o", 0, 0), ("o", 1, 0), ("o", 2, 0),
    ("sum", 0, 0), ("sum", 1, 0), ("sum", 2, 0), ("p", 0, 1), ("p", 1, 1), ("p", 2, 1), ("o", 0, 1), ("o", 1, 1),
    ("o", 2, 1), ("sum", 0, 1), ("sum", 1, 1), ("sum", 2, 1), ("mid", 0, 0), ("mid", 1, 0), ("mid", 2, 0),
    ("p", 0, 2), ("p", 1, 2), ("p", 2, 2), ("o", 0, 2), ("o", 1, 2), ("o", 2, 2), ("sum", 0, 2), ("sum", 1, 2),
    ("sum", 2, 2), ("mid", 0, 1), ("mid", 1, 1), ("mid", 2, 1), ("p", 0, 3), ("p", 1, 3), ("p", 2, 3), ("o", 0, 3),
    ("o", 1, 3), ("o", 2, 3), ("sum", 0, 3), ("sum", 1, 3), ("sum", 2, 3), ("mid", 0, 2), ("mid", 1, 2),
    ("mid", 2, 2), ("mid", 0, 3), ("mid", 1, 3), ("mid", 2, 3), ("p", 0, 4), ("o", 0, 4), ("sum", 0, 4), ("p", 1, 4),
    ("o", 1, 4), ("sum", 1, 4), ("p", 2, 4), ("o", 2, 4), ("sum", 2, 4), ("most", 0), ("most", 1), ("most", 2),
    ("fin", 0), ("fin", 1), ("fin", 2),
]


def kernel(
    q_hbm, k_hbm, v_hbm, out_hbm,
    kbuf, vbuf, qbuf, qsend, qm, kcat, sbuf, zrecv, stat, statv, pbuf, vcat, obuf, orecv, xhalf, xfull, ofin, oown,
    load_sem, k_ss, k_rs, v_ss, v_rs, qs_ss, qs_rs, qx_ss, qx_rs, qc_ss, qc_rs, z_ss, z_rs, st_ss, st_rs,
    p_ss, p_rs, o_ss, o_rs, xh_ss, xh_rs, xf_ss, xf_rs, w_ss, w_rs,
):
    s_id, r_id = lax.axis_index("seq"), lax.axis_index("res")
    z, yh = s_id // 2, s_id % 2
    yl, x, c = r_id // 8, (r_id // 2) % 4, r_id % 2
    y = yh * 4 + yl

    def at(z_=None, y_=None, x_=None, c_=None):
        z_ = z if z_ is None else z_
        y_ = y if y_ is None else y_
        x_ = x if x_ is None else x_
        c_ = c if c_ is None else c_
        return {"seq": z_ * 2 + y_ // 4, "res": ((y_ % 4) * 4 + x_) * 2 + c_}

    def zdev(k):
        return at(z_=(z + k + NZ) % NZ)

    def ydev(k):
        return at(y_=(y + k + NY) % NY)

    way_out = (yh + c) % 2
    taker = at(y_=(y + 2 - 4 * way_out + NY) % NY, c_=yh)
    way_in = ((y + 6) % NY // 4 + c) % 2
    owner = at(y_=(y - 2 + 4 * way_in + NY) % NY, c_=(c + way_in) % 2)
    sibling = at(c_=1 - c)

    def group(k):
        g = (x * 2 + c + k) % 8
        return at(x_=g // 2, c_=g % 2)

    def group_index(k):
        g = (x * 2 + c + k + 8) % 8
        return g // 2, g % 2

    def remote(src, dst, ss, rs, dev):
        return pltpu.make_async_remote_copy(
            src_ref=src, dst_ref=dst, send_sem=ss, recv_sem=rs, device_id=dev, device_id_type=pl.DeviceIdType.MESH
        )

    sent, due = {}, {}

    def go(key, send, recv=None):
        send().start()
        sent[key] = send
        due[key] = recv or send

    def got(key):
        due.pop(key)().wait_recv()

    def left(*keys):
        for key in keys:
            sent.pop(key)().wait_send()

    def lanes(p):
        return pl.ds(p * LANES, LANES)

    def load_k(p):
        return pltpu.make_async_copy(k_hbm.at[:, :, lanes(p)], kbuf.at[p, y], load_sem.at[0, p])

    def load_v(p):
        return pltpu.make_async_copy(v_hbm.at[:, :, lanes(p)], vbuf.at[p, y], load_sem.at[1, p])

    def load_q(p):
        return pltpu.make_async_copy(q_hbm.at[:, :, lanes(p)], qsend.at[p], load_sem.at[2, p])

    def ring(buf, ss, rs, p, step, way):
        src = (y - way * (step - 1) + NY) % NY
        half = pl.ds(0, ROWS) if step < 4 else (pl.ds(0, 2) if way == 1 else pl.ds(2, 2))
        d = 0 if way == 1 else 1
        view = buf.at[p, src, half]
        return remote(view, view, ss.at[p, step - 1, d], rs.at[p, step - 1, d], ydev(way))

    def ring_recv(buf, ss, rs, p, step, way):
        src = (y - way * step + NY) % NY
        half = pl.ds(0, ROWS) if step < 4 else (pl.ds(0, 2) if way == 1 else pl.ds(2, 2))
        d = 0 if way == 1 else 1
        view = buf.at[p, src, half]
        return remote(view, view, ss.at[p, step - 1, d], rs.at[p, step - 1, d], ydev(way))

    K = (kbuf, k_ss, k_rs)
    V = (vbuf, v_ss, v_rs)

    def ring_start(t, p, step):
        for way in (1, -1):
            go((t is K, p, step, way), functools.partial(ring, *t, p, step, way), functools.partial(ring_recv, *t, p, step, way))

    def ring_wait(t, p, step):
        for way in (1, -1):
            got((t is K, p, step, way))

    def q_move(p, slot, dev):
        return remote(qsend.at[p], qbuf.at[p, slot, x], qs_ss.at[p], qs_rs.at[p], dev)

    def q_start(p):
        load_q(p).wait()
        go(("qs", p), lambda: q_move(p, yh, taker), lambda: q_move(p, c, taker))

    def q_ring(p, step, way, behind):
        d = 0 if way == 1 else 1
        half = pl.ds(0, ROWS) if step == 1 else pl.ds(2 * d, 2)
        view = qbuf.at[p, c, (x - way * (step - 1 + behind) + NX) % NX, half]
        return remote(view, view, qx_ss.at[p, step - 1, d], qx_rs.at[p, step - 1, d], at(x_=(x + way + NX) % NX))

    def q_ring_start(p, step):
        for way in (1, -1):
            go(("qx", p, step, way), functools.partial(q_ring, p, step, way, 0), functools.partial(q_ring, p, step, way, 1))

    def q_step(p, step):
        if step == 0:
            got(("qs", p))
        else:
            for way in (1, -1):
                got(("qx", p, step, way))
        if step < 2:
            q_ring_start(p, step + 1)
        else:
            go(("qc", p), functools.partial(q_share, p), functools.partial(q_share_recv, p))

    def q_share(p):
        return remote(qbuf.at[p, c], qbuf.at[p, c], qc_ss.at[p], qc_rs.at[p], sibling)

    def q_share_recv(p):
        return remote(qbuf.at[p, 1 - c], qbuf.at[p, 1 - c], qc_ss.at[p], qc_rs.at[p], sibling)

    def q_spread_start(p, where):
        if where is at_home:
            at_home(lambda: load_q_home(p).wait())
        else:
            got(("qs", p))
        for k in (2, 1, 3):
            go(("qx", p, k, where), functools.partial(q_spread, p, k), functools.partial(q_spread_recv, p, k), where)

    lane = lax.broadcasted_iota(jnp.int32, (HALF, LANES), 1)

    def q_build(p):
        got(("qc", p))
        for g in range(2):
            for r in range(ROWS):
                cols = pl.ds((g * ROWS + r) * LANES, LANES)
                block = qbuf[p, g, :, r].astype(F32)
                for s in range(NZ):
                    part = jnp.concatenate([block[i, s * EIGHT : (s + 1) * EIGHT] for i in range(NX)], axis=0)
                    zero = jnp.zeros_like(part)
                    qm[p, s, 0, :, cols] = jnp.where(lane < 64, part, zero).astype(BF16)
                    qm[p, s, 1, :, cols] = jnp.where(lane >= 64, part, zero).astype(BF16)

    def scores(p):
        ring_wait(K, p, 4)
        for g in range(2):
            for r in range(ROWS):
                cols = pl.ds((g * ROWS + r) * LANES, LANES)
                kcat[:, cols] = kbuf[p, g * 4 : g * 4 + 4, r].reshape(256, LANES)
        for half in range(2):
            part = lax.dot_general(
                qm[p, half * 4 : half * 4 + 4].reshape(256, 1024), kcat[...], (((1,), (1,)), ((), ())), preferred_element_type=F32
            )
            sbuf[p, half * 4 : half * 4 + 4] = part.reshape(4, TOK, 256)
        z_start(p, 1)

    def zslice(way, step):
        return (z + way * (5 - step) + NZ) % NZ

    def z_copy(p, step, way):
        d = 0 if way == 1 else 1
        half = pl.ds(0, TOK) if step > 1 else pl.ds(d * 32, 32)
        return remote(
            sbuf.at[p, zslice(way, step), half],
            zrecv.at[p, d, step - 1, half],
            z_ss.at[p, step - 1, d],
            z_rs.at[p, step - 1, d],
            zdev(way),
        )

    def z_start(p, step):
        for way in (1, -1):
            go(("z", p, step, way), functools.partial(z_copy, p, step, way))

    def z_add(p, step):
        for way in (1, -1):
            d = 0 if way == 1 else 1
            got(("z", p, step, way))
            s = zslice(way, step + 1)
            if step == 1:
                rows = pl.ds(d * 32, 32)
                sbuf[p, s, rows] = sbuf[p, s, rows] + zrecv[p, d, 0, rows]
            else:
                sbuf[p, s] = sbuf[p, s] + zrecv[p, d, step - 1]
        z_start(p, step + 1)

    def stat_copy(p, k):
        return remote(stat.at[p, 0], stat.at[p, k], st_ss.at[p, k - 1], st_rs.at[p, k - 1], group(k))

    def softmax_local(p):
        for way in (1, -1):
            got(("z", p, 4, way))
        s = sbuf[p, z] + zrecv[p, 0, 3] + zrecv[p, 1, 3]
        s = s * (1.0 / 64.0)
        m = jnp.max(s, axis=1, keepdims=True)
        e = jnp.exp(s - m)
        l = jnp.sum(e, axis=1, keepdims=True)
        statv[p] = e
        col = lax.broadcasted_iota(jnp.int32, (TOK, LANES), 1)
        both = jnp.where(col == 0, m, l)
        tall = jnp.concatenate([both, both], axis=0)
        stat[p, 0] = jnp.transpose(tall)[0:8, :]
        for k in range(1, 8):
            go(("st", p, k), functools.partial(stat_copy, p, k))

    def softmax_global(p):
        for k in range(1, 8):
            got(("st", p, k))
        m = stat[p, 0, 0:1, :]
        for k in range(1, 8):
            m = jnp.maximum(m, stat[p, k, 0:1, :])
        l = jnp.zeros_like(m)
        for k in range(8):
            l = l + jnp.exp(stat[p, k, 0:1, :] - m) * stat[p, k, 1:2, :]
        factor = jnp.exp(stat[p, 0, 0:1, :] - m) / l
        tall = jnp.transpose(jnp.broadcast_to(factor, (LANES, LANES)))
        pbuf[p, z] = (statv[p] * tall[0:TOK, 0:1]).astype(BF16)
        p_start(p, 1)

    def p_view(p, step, way, slot):
        half = pl.ds(0, TOK) if step < 4 else pl.ds(0 if way == 1 else 32, 32)
        return pbuf.at[p, (slot + 2 * NZ) % NZ, half]

    def p_copy(p, step, way, behind):
        d = 0 if way == 1 else 1
        view = p_view(p, step, way, z - way * (step - 1 + behind))
        return remote(view, view, p_ss.at[p, step - 1, d], p_rs.at[p, step - 1, d], zdev(way))

    def p_start(p, step):
        for way in (1, -1):
            go(("p", p, step, way), functools.partial(p_copy, p, step, way, 0), functools.partial(p_copy, p, step, way, 1))

    def p_wait(p, step):
        for way in (1, -1):
            got(("p", p, step, way))

    def v_build(p):
        ring_wait(V, p, 4)
        for g in range(2):
            for r in range(ROWS):
                vcat[p, g, :, pl.ds(r * LANES, LANES)] = vbuf[p, g * 4 : g * 4 + 4, r].reshape(256, LANES)

    first = lax.broadcasted_iota(jnp.int32, (HALF, ROWS * LANES), 1) % LANES < 64

    def slices(k):
        if k == 0:
            return [z]
        if k == 4:
            return [(z + 4) % NZ]
        return [(z + NZ - k) % NZ, (z + k) % NZ]

    def line(k):
        return pl.ds(0, 1) if k == 0 else pl.ds(2 * k - 1, 1 if k == 4 else 2)

    def places(k):
        return range(line(k).start, line(k).start + line(k).size)

    def o_copy(p, k):
        return remote(obuf.at[p, 1 - c, line(k)], orecv.at[p, line(k)], o_ss.at[p, k], o_rs.at[p, k], sibling)

    def x_half(p, k, way):
        d = 0 if way == 1 else 1
        return remote(
            obuf.at[p, c, line(k), (x + 2) % NX, :, pl.ds(256 * d, 256)], xhalf.at[p, d, line(k)],
            xh_ss.at[p, k, d], xh_rs.at[p, k, d], at(x_=(x + way + NX) % NX),
        )

    def x_full(p, k, way):
        d = (1, -1, 2).index(way)
        to = (x + way + NX) % NX
        return remote(obuf.at[p, c, line(k), to], xfull.at[p, d, line(k)], xf_ss.at[p, k, d], xf_rs.at[p, k, d], at(x_=to))

    def attend(p, k):
        parts = slices(k)
        probs = [pbuf[p, s] for s in parts]
        probs = probs[0] if len(probs) == 1 else jnp.concatenate(probs, axis=0)
        for g in (1 - c, c):
            o = lax.dot_general(probs, vcat[p, g], (((1,), (0,)), ((), ())), preferred_element_type=F32)
            for t in range(len(parts)):
                both = jnp.where(first, o[t * TOK : t * TOK + HALF], o[t * TOK + HALF : (t + 1) * TOK])
                obuf[p, g, line(k).start + t] = both.reshape(NX, EIGHT, ROWS * LANES)
            if g is not c:
                go(("o", p, k), functools.partial(o_copy, p, k))

    def chip_sum(p, k):
        got(("o", p, k))
        for n in places(k):
            obuf[p, c, n] = obuf[p, c, n] + orecv[p, n]
        if k == 4:
            for way in (2, 1, -1):
                go(("xf", p, k, way), functools.partial(x_full, p, k, way))
            return
        for way in (1, -1):
            go(("xh", p, k, way), functools.partial(x_half, p, k, way))

    def x_sum(p, k):
        for way in (1, -1):
            d = 0 if way == 1 else 1
            got(("xh", p, k, way))
            to = (x + way + NX) % NX
            cols = pl.ds(256 * d, 256)
            for n in places(k):
                obuf[p, c, n, to, :, cols] = obuf[p, c, n, to, :, cols] + xhalf[p, d, n]
            go(("xf", p, k, way), functools.partial(x_full, p, k, way))

    def w_copy(p, i):
        rows = pl.ds(pl.multiple_of(((z + 4) % NZ // 2 + i) % NX * 16, 16), 16)
        return remote(oown.at[p, :, rows], out_hbm.at[:, rows, lanes(p)], w_ss.at[p, i], w_rs.at[p, i], owner)

    def totals(p, k):
        for way in (1, -1) if k < 4 else (1, -1, 2):
            got(("xf", p, k, way))
        for t, s in enumerate(slices(k)):
            n = line(k).start + t
            total = obuf[p, c, n, x] + xfull[p, 0, n] + xfull[p, 1, n]
            ofin[p, s] = total if k < 4 else total + xfull[p, 2, n]

    def w_start(p, i):
        g = ((z + 4) % NZ // 2 + i) % NX
        rows = pl.ds(pl.multiple_of(g * 16, 16), 16)
        both = ofin[p, pl.ds(g * 2, 2)].reshape(16, ROWS * LANES)
        for r in range(ROWS):
            oown[p, r, rows, :] = both[:, r * LANES : (r + 1) * LANES].astype(BF16)
        go(("w", p, i), functools.partial(w_copy, p, i))

    def finish_most(p):
        for k in range(4):
            totals(p, k)
        for i in (1, 2, 3):
            w_start(p, i)

    def finish(p):
        totals(p, 4)
        w_start(p, 0)

    pairs = range(PAIRS)
    for p in pairs:
        load_q(p).start()
        load_k(p).start()
    barrier = pltpu.get_barrier_semaphore()
    peers = [zdev(1), zdev(-1), ydev(1), ydev(-1), taker, owner] + [group(k) for k in range(1, 8)]
    for dev in peers:
        pl.semaphore_signal(barrier, inc=1, device_id=dev, device_id_type=pl.DeviceIdType.MESH)
    pl.semaphore_wait(barrier, len(peers))

    def schedule():
        def k_step(p, step):
            ring_wait(K, p, step)
            ring_start(K, p, step + 1)

        def v_step(p, step):
            ring_wait(V, p, step)
            ring_start(V, p, step + 1)

        def k_first(p):
            load_k(p).wait()
            ring_start(K, p, 1)

        def v_first(p):
            load_v(p).wait()
            ring_start(V, p, 1)

        def p_step(p, k):
            p_wait(p, k)
            if k < 4:
                p_start(p, k + 1)

        act = dict(
            q0=q_start, q=q_step, build=q_build, k1=k_first, k=k_step, s=scores, z=z_add, local=softmax_local,
            soft=softmax_global, v1=v_first, v=v_step, vcat=v_build, p=p_step, o=attend, sum=chip_sum, mid=x_sum,
            vl=lambda p: load_v(p).start(), most=finish_most, fin=finish, qw=lambda p: left(("qs", p)), kw=lambda p: left((True, p, 1, 1), (True, p, 1, -1)),
            pw=lambda p: left(("p", p, 1, 1), ("p", p, 1, -1)),
        )
        for name, *arg in ORDER:
            act[name](*arg)

    schedule()

    for copy in due.values():
        copy().wait_recv()
    for copy in sent.values():
        copy().wait_send()


def local(queries, keys, values):
    vmem = pltpu.VMEM
    dma = pltpu.SemaphoreType.DMA
    block = (ROWS, TOK, LANES)
    return pl.pallas_call(
        kernel,
        out_shape=jax.ShapeDtypeStruct(queries.shape, BF16),
        in_specs=[pl.BlockSpec(memory_space=pl.ANY)] * 3,
        out_specs=pl.BlockSpec(memory_space=pl.ANY),
        scratch_shapes=[
            vmem((PAIRS, NY) + block, BF16),
            vmem((PAIRS, NY) + block, BF16),
            vmem((PAIRS, 2, NX) + block, BF16),
            vmem((PAIRS,) + block, BF16),
            vmem((PAIRS, NZ, 2, HALF, 1024), BF16),
            vmem((256, 1024), BF16),
            vmem((PAIRS, NZ, TOK, 256), F32),
            vmem((PAIRS, 2, 4, TOK, 256), F32),
            vmem((PAIRS, 8, 8, LANES), F32),
            vmem((PAIRS, TOK, 256), F32),
            vmem((PAIRS, NZ, TOK, 256), BF16),
            vmem((PAIRS, 2, 256, 512), BF16),
            vmem((PAIRS, 2, NZ, NX, EIGHT, 512), F32),
            vmem((PAIRS, NZ, NX, EIGHT, 512), F32),
            vmem((PAIRS, 2, NZ, EIGHT, 256), F32),
            vmem((PAIRS, 3, NZ, EIGHT, 512), F32),
            vmem((PAIRS, NZ, EIGHT, 512), F32),
            vmem((PAIRS,) + block, BF16),
            dma((3, PAIRS)),
            dma((PAIRS, 4, 2)), dma((PAIRS, 4, 2)),
            dma((PAIRS, 4, 2)), dma((PAIRS, 4, 2)),
            dma((PAIRS,)), dma((PAIRS,)),
            dma((PAIRS, 2, 2)), dma((PAIRS, 2, 2)),
            dma((PAIRS,)), dma((PAIRS,)),
            dma((PAIRS, 4, 2)), dma((PAIRS, 4, 2)),
            dma((PAIRS, 7)), dma((PAIRS, 7)),
            dma((PAIRS, 4, 2)), dma((PAIRS, 4, 2)),
            dma((PAIRS, 5)), dma((PAIRS, 5)),
            dma((PAIRS, 5, 2)), dma((PAIRS, 5, 2)),
            dma((PAIRS, 5, 3)), dma((PAIRS, 5, 3)),
            dma((PAIRS, 4)), dma((PAIRS, 4)),
        ],
        compiler_params=pltpu.CompilerParams(collective_id=0, has_side_effects=True, vmem_limit_bytes=63 << 20),
    )(queries, keys, values)


def solution(mesh):
    spec = P("seq", "res", None)
    return jax.shard_map(local, mesh=mesh, in_specs=(spec, spec, spec), out_specs=spec, check_vma=False)
```

```python
import functools

import jax
import jax.numpy as jnp
from jax import lax
from jax.experimental import pallas as pl
from jax.experimental.pallas import tpu as pltpu
from jax.sharding import PartitionSpec as P

NZ, NY, NX = 8, 8, 4
PAIRS = 3
ROWS, TOK, LANES = 4, 64, 128
EIGHT = TOK // NZ
HALF = NX * EIGHT
F32, BF16 = jnp.float32, jnp.bfloat16


ORDER = [
    ("q0", 0), ("q0", 1), ("q0", 2), ("qw", 0), ("qw", 1), ("qw", 2), ("k1", 0), ("k1", 1), ("k1", 2), ("vl", 0),
    ("vl", 1), ("vl", 2), ("q", 0, 0), ("q", 1, 0), ("q", 2, 0), ("k", 0, 1), ("k", 1, 1), ("k", 2, 1), ("q", 0, 1),
    ("q", 1, 1), ("q", 2, 1), ("k", 0, 2), ("k", 1, 2), ("k", 2, 2), ("q", 0, 2), ("q", 1, 2), ("q", 2, 2),
    ("k", 0, 3), ("k", 1, 3), ("k", 2, 3), ("v1", 0), ("v1", 1), ("v1", 2), ("build", 0), ("build", 1), ("build", 2),
    ("s", 0), ("s", 1), ("s", 2), ("z", 0, 1), ("z", 1, 1), ("z", 2, 1), ("v", 0, 1), ("v", 1, 1), ("v", 2, 1),
    ("z", 0, 2), ("z", 1, 2), ("z", 2, 2), ("v", 0, 2), ("v", 1, 2), ("v", 2, 2), ("z", 0, 3), ("z", 1, 3),
    ("z", 2, 3), ("v", 0, 3), ("v", 1, 3), ("v", 2, 3), ("local", 0), ("local", 1), ("local", 2), ("soft", 0),
    ("soft", 1), ("soft", 2), ("vcat", 0), ("vcat", 1), ("vcat", 2), ("o", 0, 0), ("o", 1, 0), ("o", 2, 0),
    ("sum", 0, 0), ("sum", 1, 0), ("sum", 2, 0), ("p", 0, 1), ("p", 1, 1), ("p", 2, 1), ("o", 0, 1), ("o", 1, 1),
    ("o", 2, 1), ("sum", 0, 1), ("sum", 1, 1), ("sum", 2, 1), ("mid", 0, 0), ("mid", 1, 0), ("mid", 2, 0),
    ("p", 0, 2), ("p", 1, 2), ("p", 2, 2), ("o", 0, 2), ("o", 1, 2), ("o", 2, 2), ("sum", 0, 2), ("sum", 1, 2),
    ("sum", 2, 2), ("mid", 0, 1), ("mid", 1, 1), ("mid", 2, 1), ("p", 0, 3), ("p", 1, 3), ("p", 2, 3), ("o", 0, 3),
    ("o", 1, 3), ("o", 2, 3), ("sum", 0, 3), ("sum", 1, 3), ("sum", 2, 3), ("mid", 0, 2), ("mid", 1, 2),
    ("mid", 2, 2), ("p", 0, 4), ("o", 0, 4), ("sum", 0, 4), ("p", 1, 4),
    ("o", 1, 4), ("sum", 1, 4), ("p", 2, 4), ("o", 2, 4), ("sum", 2, 4), ("most", 0), ("most", 1), ("most", 2),
    ("fin", 0), ("fin", 1), ("fin", 2),
]


def kernel(
    q_hbm, k_hbm, v_hbm, out_hbm,
    kbuf, vbuf, qbuf, qsend, qm, kcat, sbuf, zrecv, stat, statv, pbuf, vcat, obuf, orecv, xhalf, xfull, ofin, oown,
    load_sem, k_ss, k_rs, v_ss, v_rs, qs_ss, qs_rs, qx_ss, qx_rs, qc_ss, qc_rs, z_ss, z_rs, st_ss, st_rs,
    p_ss, p_rs, o_ss, o_rs, xh_ss, xh_rs, xf_ss, xf_rs, w_ss, w_rs,
):
    s_id, r_id = lax.axis_index("seq"), lax.axis_index("res")
    z, yh = s_id // 2, s_id % 2
    yl, x, c = r_id // 8, (r_id // 2) % 4, r_id % 2
    y = yh * 4 + yl

    def at(z_=None, y_=None, x_=None, c_=None):
        z_ = z if z_ is None else z_
        y_ = y if y_ is None else y_
        x_ = x if x_ is None else x_
        c_ = c if c_ is None else c_
        return {"seq": z_ * 2 + y_ // 4, "res": ((y_ % 4) * 4 + x_) * 2 + c_}

    def zdev(k):
        return at(z_=(z + k + NZ) % NZ)

    def ydev(k):
        return at(y_=(y + k + NY) % NY)

    way_out = (yh + c) % 2
    taker = at(y_=(y + 2 - 4 * way_out + NY) % NY, c_=yh)
    way_in = ((y + 6) % NY // 4 + c) % 2
    owner = at(y_=(y - 2 + 4 * way_in + NY) % NY, c_=(c + way_in) % 2)
    sibling = at(c_=1 - c)

    def group(k):
        g = (x * 2 + c + k) % 8
        return at(x_=g // 2, c_=g % 2)

    def group_index(k):
        g = (x * 2 + c + k + 8) % 8
        return g // 2, g % 2

    def remote(src, dst, ss, rs, dev):
        return pltpu.make_async_remote_copy(
            src_ref=src, dst_ref=dst, send_sem=ss, recv_sem=rs, device_id=dev, device_id_type=pl.DeviceIdType.MESH
        )

    sent, due = {}, {}

    def go(key, send, recv=None):
        send().start()
        sent[key] = send
        due[key] = recv or send

    def got(key):
        due.pop(key)().wait_recv()

    def left(*keys):
        for key in keys:
            sent.pop(key)().wait_send()

    def lanes(p):
        return pl.ds(p * LANES, LANES)

    def load_k(p):
        return pltpu.make_async_copy(k_hbm.at[:, :, lanes(p)], kbuf.at[p, y], load_sem.at[0, p])

    def load_v(p):
        return pltpu.make_async_copy(v_hbm.at[:, :, lanes(p)], vbuf.at[p, y], load_sem.at[1, p])

    def load_q(p):
        return pltpu.make_async_copy(q_hbm.at[:, :, lanes(p)], qsend.at[p], load_sem.at[2, p])

    def ring(buf, ss, rs, p, step, way):
        src = (y - way * (step - 1) + NY) % NY
        half = pl.ds(0, ROWS) if step < 4 else (pl.ds(0, 2) if way == 1 else pl.ds(2, 2))
        d = 0 if way == 1 else 1
        view = buf.at[p, src, half]
        return remote(view, view, ss.at[p, step - 1, d], rs.at[p, step - 1, d], ydev(way))

    def ring_recv(buf, ss, rs, p, step, way):
        src = (y - way * step + NY) % NY
        half = pl.ds(0, ROWS) if step < 4 else (pl.ds(0, 2) if way == 1 else pl.ds(2, 2))
        d = 0 if way == 1 else 1
        view = buf.at[p, src, half]
        return remote(view, view, ss.at[p, step - 1, d], rs.at[p, step - 1, d], ydev(way))

    K = (kbuf, k_ss, k_rs)
    V = (vbuf, v_ss, v_rs)

    def ring_start(t, p, step):
        for way in (1, -1):
            go((t is K, p, step, way), functools.partial(ring, *t, p, step, way), functools.partial(ring_recv, *t, p, step, way))

    def ring_wait(t, p, step):
        for way in (1, -1):
            got((t is K, p, step, way))

    def q_move(p, slot, dev):
        return remote(qsend.at[p], qbuf.at[p, slot, x], qs_ss.at[p], qs_rs.at[p], dev)

    def q_start(p):
        load_q(p).wait()
        go(("qs", p), lambda: q_move(p, yh, taker), lambda: q_move(p, c, taker))

    def q_ring(p, step, way, behind):
        d = 0 if way == 1 else 1
        half = pl.ds(0, ROWS) if step == 1 else pl.ds(2 * d, 2)
        view = qbuf.at[p, c, (x - way * (step - 1 + behind) + NX) % NX, half]
        return remote(view, view, qx_ss.at[p, step - 1, d], qx_rs.at[p, step - 1, d], at(x_=(x + way + NX) % NX))

    def q_ring_start(p, step):
        for way in (1, -1):
            go(("qx", p, step, way), functools.partial(q_ring, p, step, way, 0), functools.partial(q_ring, p, step, way, 1))

    def q_step(p, step):
        if step == 0:
            got(("qs", p))
        else:
            for way in (1, -1):
                got(("qx", p, step, way))
        if step < 2:
            q_ring_start(p, step + 1)
        else:
            go(("qc", p), functools.partial(q_share, p), functools.partial(q_share_recv, p))

    def q_share(p):
        return remote(qbuf.at[p, c], qbuf.at[p, c], qc_ss.at[p], qc_rs.at[p], sibling)

    def q_share_recv(p):
        return remote(qbuf.at[p, 1 - c], qbuf.at[p, 1 - c], qc_ss.at[p], qc_rs.at[p], sibling)

    def q_spread_start(p, where):
        if where is at_home:
            at_home(lambda: load_q_home(p).wait())
        else:
            got(("qs", p))
        for k in (2, 1, 3):
            go(("qx", p, k, where), functools.partial(q_spread, p, k), functools.partial(q_spread_recv, p, k), where)

    lane = lax.broadcasted_iota(jnp.int32, (HALF, LANES), 1)

    def q_build(p):
        got(("qc", p))
        for g in range(2):
            for r in range(ROWS):
                cols = pl.ds((g * ROWS + r) * LANES, LANES)
                block = qbuf[p, g, :, r].astype(F32)
                for s in range(NZ):
                    part = jnp.concatenate([block[i, s * EIGHT : (s + 1) * EIGHT] for i in range(NX)], axis=0)
                    zero = jnp.zeros_like(part)
                    qm[p, s, 0, :, cols] = jnp.where(lane < 64, part, zero).astype(BF16)
                    qm[p, s, 1, :, cols] = jnp.where(lane >= 64, part, zero).astype(BF16)

    def scores(p):
        ring_wait(K, p, 4)
        for g in range(2):
            for r in range(ROWS):
                cols = pl.ds((g * ROWS + r) * LANES, LANES)
                kcat[:, cols] = kbuf[p, g * 4 : g * 4 + 4, r].reshape(256, LANES)
        for half in range(2):
            part = lax.dot_general(
                qm[p, half * 4 : half * 4 + 4].reshape(256, 1024), kcat[...], (((1,), (1,)), ((), ())), preferred_element_type=F32
            )
            sbuf[p, half * 4 : half * 4 + 4] = part.reshape(4, TOK, 256)
        z_start(p, 1)

    def zslice(way, step):
        return (z + way * (5 - step) + NZ) % NZ

    def z_copy(p, step, way):
        d = 0 if way == 1 else 1
        half = pl.ds(0, TOK) if step > 1 else pl.ds(d * 32, 32)
        return remote(
            sbuf.at[p, zslice(way, step), half],
            zrecv.at[p, d, step - 1, half],
            z_ss.at[p, step - 1, d],
            z_rs.at[p, step - 1, d],
            zdev(way),
        )

    def z_start(p, step):
        for way in (1, -1):
            go(("z", p, step, way), functools.partial(z_copy, p, step, way))

    def z_add(p, step):
        for way in (1, -1):
            d = 0 if way == 1 else 1
            got(("z", p, step, way))
            s = zslice(way, step + 1)
            if step == 1:
                rows = pl.ds(d * 32, 32)
                sbuf[p, s, rows] = sbuf[p, s, rows] + zrecv[p, d, 0, rows]
            else:
                sbuf[p, s] = sbuf[p, s] + zrecv[p, d, step - 1]
        z_start(p, step + 1)

    def stat_copy(p, k):
        return remote(stat.at[p, 0], stat.at[p, k], st_ss.at[p, k - 1], st_rs.at[p, k - 1], group(k))

    def softmax_local(p):
        for way in (1, -1):
            got(("z", p, 4, way))
        s = sbuf[p, z] + zrecv[p, 0, 3] + zrecv[p, 1, 3]
        s = s * (1.0 / 64.0)
        m = jnp.max(s, axis=1, keepdims=True)
        e = jnp.exp(s - m)
        l = jnp.sum(e, axis=1, keepdims=True)
        statv[p] = e
        col = lax.broadcasted_iota(jnp.int32, (TOK, LANES), 1)
        both = jnp.where(col == 0, m, l)
        tall = jnp.concatenate([both, both], axis=0)
        stat[p, 0] = jnp.transpose(tall)[0:8, :]
        for k in range(1, 8):
            go(("st", p, k), functools.partial(stat_copy, p, k))

    def softmax_global(p):
        for k in range(1, 8):
            got(("st", p, k))
        m = stat[p, 0, 0:1, :]
        for k in range(1, 8):
            m = jnp.maximum(m, stat[p, k, 0:1, :])
        l = jnp.zeros_like(m)
        for k in range(8):
            l = l + jnp.exp(stat[p, k, 0:1, :] - m) * stat[p, k, 1:2, :]
        factor = jnp.exp(stat[p, 0, 0:1, :] - m) / l
        tall = jnp.transpose(jnp.broadcast_to(factor, (LANES, LANES)))
        pbuf[p, z] = (statv[p] * tall[0:TOK, 0:1]).astype(BF16)
        p_start(p, 1)

    def p_view(p, step, way, slot):
        half = pl.ds(0, TOK) if step < 4 else pl.ds(0 if way == 1 else 32, 32)
        return pbuf.at[p, (slot + 2 * NZ) % NZ, half]

    def p_copy(p, step, way, behind):
        d = 0 if way == 1 else 1
        view = p_view(p, step, way, z - way * (step - 1 + behind))
        return remote(view, view, p_ss.at[p, step - 1, d], p_rs.at[p, step - 1, d], zdev(way))

    def p_start(p, step):
        for way in (1, -1):
            go(("p", p, step, way), functools.partial(p_copy, p, step, way, 0), functools.partial(p_copy, p, step, way, 1))

    def p_wait(p, step):
        for way in (1, -1):
            got(("p", p, step, way))

    def v_build(p):
        ring_wait(V, p, 4)
        for g in range(2):
            for r in range(ROWS):
                vcat[p, g, :, pl.ds(r * LANES, LANES)] = vbuf[p, g * 4 : g * 4 + 4, r].reshape(256, LANES)

    first = lax.broadcasted_iota(jnp.int32, (HALF, ROWS * LANES), 1) % LANES < 64

    def slices(k):
        if k == 0:
            return [z]
        if k == 4:
            return [(z + 4) % NZ]
        return [(z + NZ - k) % NZ, (z + k) % NZ]

    def line(k):
        return pl.ds(0, 1) if k == 0 else pl.ds(2 * k - 1, 1 if k == 4 else 2)

    def places(k):
        return range(line(k).start, line(k).start + line(k).size)

    def o_copy(p, k):
        return remote(obuf.at[p, 1 - c, line(k)], orecv.at[p, line(k)], o_ss.at[p, k], o_rs.at[p, k], sibling)

    def x_half(p, k, way):
        d = 0 if way == 1 else 1
        return remote(
            obuf.at[p, c, line(k), (x + 2) % NX, :, pl.ds(256 * d, 256)], xhalf.at[p, d, line(k)],
            xh_ss.at[p, k, d], xh_rs.at[p, k, d], at(x_=(x + way + NX) % NX),
        )

    def x_full(p, k, way):
        d = (1, -1, 2).index(way)
        to = (x + way + NX) % NX
        return remote(obuf.at[p, c, line(k), to], xfull.at[p, d, line(k)], xf_ss.at[p, k, d], xf_rs.at[p, k, d], at(x_=to))

    def attend(p, k):
        parts = slices(k)
        probs = [pbuf[p, s] for s in parts]
        probs = probs[0] if len(probs) == 1 else jnp.concatenate(probs, axis=0)
        for g in (1 - c, c):
            o = lax.dot_general(probs, vcat[p, g], (((1,), (0,)), ((), ())), preferred_element_type=F32)
            for t in range(len(parts)):
                both = jnp.where(first, o[t * TOK : t * TOK + HALF], o[t * TOK + HALF : (t + 1) * TOK])
                obuf[p, g, line(k).start + t] = both.reshape(NX, EIGHT, ROWS * LANES)
            if g is not c:
                go(("o", p, k), functools.partial(o_copy, p, k))

    def chip_sum(p, k):
        got(("o", p, k))
        for n in places(k):
            obuf[p, c, n] = obuf[p, c, n] + orecv[p, n]
        if k > 2:
            for way in (2, 1, -1):
                go(("xf", p, k, way), functools.partial(x_full, p, k, way))
            return
        for way in (1, -1):
            go(("xh", p, k, way), functools.partial(x_half, p, k, way))

    def x_sum(p, k):
        for way in (1, -1):
            d = 0 if way == 1 else 1
            got(("xh", p, k, way))
            to = (x + way + NX) % NX
            cols = pl.ds(256 * d, 256)
            for n in places(k):
                obuf[p, c, n, to, :, cols] = obuf[p, c, n, to, :, cols] + xhalf[p, d, n]
            go(("xf", p, k, way), functools.partial(x_full, p, k, way))

    def w_copy(p, i):
        rows = pl.ds(pl.multiple_of(((z + 4) % NZ // 2 + i) % NX * 16, 16), 16)
        return remote(oown.at[p, :, rows], out_hbm.at[:, rows, lanes(p)], w_ss.at[p, i], w_rs.at[p, i], owner)

    def totals(p, k):
        for way in (1, -1) if k < 3 else (1, -1, 2):
            got(("xf", p, k, way))
        for t, s in enumerate(slices(k)):
            n = line(k).start + t
            total = obuf[p, c, n, x] + xfull[p, 0, n] + xfull[p, 1, n]
            ofin[p, s] = total if k < 3 else total + xfull[p, 2, n]

    def w_start(p, i):
        g = ((z + 4) % NZ // 2 + i) % NX
        rows = pl.ds(pl.multiple_of(g * 16, 16), 16)
        both = ofin[p, pl.ds(g * 2, 2)].reshape(16, ROWS * LANES)
        for r in range(ROWS):
            oown[p, r, rows, :] = both[:, r * LANES : (r + 1) * LANES].astype(BF16)
        go(("w", p, i), functools.partial(w_copy, p, i))

    def finish_most(p):
        for k in range(4):
            totals(p, k)
        for i in (1, 2, 3):
            w_start(p, i)

    def finish(p):
        totals(p, 4)
        w_start(p, 0)

    pairs = range(PAIRS)
    for p in pairs:
        load_q(p).start()
        load_k(p).start()
    barrier = pltpu.get_barrier_semaphore()
    peers = [zdev(1), zdev(-1), ydev(1), ydev(-1), taker, owner] + [group(k) for k in range(1, 8)]
    for dev in peers:
        pl.semaphore_signal(barrier, inc=1, device_id=dev, device_id_type=pl.DeviceIdType.MESH)
    pl.semaphore_wait(barrier, len(peers))

    def schedule():
        def k_step(p, step):
            ring_wait(K, p, step)
            ring_start(K, p, step + 1)

        def v_step(p, step):
            ring_wait(V, p, step)
            ring_start(V, p, step + 1)

        def k_first(p):
            load_k(p).wait()
            ring_start(K, p, 1)

        def v_first(p):
            load_v(p).wait()
            ring_start(V, p, 1)

        def p_step(p, k):
            p_wait(p, k)
            if k < 4:
                p_start(p, k + 1)

        act = dict(
            q0=q_start, q=q_step, build=q_build, k1=k_first, k=k_step, s=scores, z=z_add, local=softmax_local,
            soft=softmax_global, v1=v_first, v=v_step, vcat=v_build, p=p_step, o=attend, sum=chip_sum, mid=x_sum,
            vl=lambda p: load_v(p).start(), most=finish_most, fin=finish, qw=lambda p: left(("qs", p)), kw=lambda p: left((True, p, 1, 1), (True, p, 1, -1)),
            pw=lambda p: left(("p", p, 1, 1), ("p", p, 1, -1)),
        )
        for name, *arg in ORDER:
            act[name](*arg)

    schedule()

    for copy in due.values():
        copy().wait_recv()
    for copy in sent.values():
        copy().wait_send()


def local(queries, keys, values):
    vmem = pltpu.VMEM
    dma = pltpu.SemaphoreType.DMA
    block = (ROWS, TOK, LANES)
    return pl.pallas_call(
        kernel,
        out_shape=jax.ShapeDtypeStruct(queries.shape, BF16),
        in_specs=[pl.BlockSpec(memory_space=pl.ANY)] * 3,
        out_specs=pl.BlockSpec(memory_space=pl.ANY),
        scratch_shapes=[
            vmem((PAIRS, NY) + block, BF16),
            vmem((PAIRS, NY) + block, BF16),
            vmem((PAIRS, 2, NX) + block, BF16),
            vmem((PAIRS,) + block, BF16),
            vmem((PAIRS, NZ, 2, HALF, 1024), BF16),
            vmem((256, 1024), BF16),
            vmem((PAIRS, NZ, TOK, 256), F32),
            vmem((PAIRS, 2, 4, TOK, 256), F32),
            vmem((PAIRS, 8, 8, LANES), F32),
            vmem((PAIRS, TOK, 256), F32),
            vmem((PAIRS, NZ, TOK, 256), BF16),
            vmem((PAIRS, 2, 256, 512), BF16),
            vmem((PAIRS, 2, NZ, NX, EIGHT, 512), F32),
            vmem((PAIRS, NZ, NX, EIGHT, 512), F32),
            vmem((PAIRS, 2, NZ, EIGHT, 256), F32),
            vmem((PAIRS, 3, NZ, EIGHT, 512), F32),
            vmem((PAIRS, NZ, EIGHT, 512), F32),
            vmem((PAIRS,) + block, BF16),
            dma((3, PAIRS)),
            dma((PAIRS, 4, 2)), dma((PAIRS, 4, 2)),
            dma((PAIRS, 4, 2)), dma((PAIRS, 4, 2)),
            dma((PAIRS,)), dma((PAIRS,)),
            dma((PAIRS, 2, 2)), dma((PAIRS, 2, 2)),
            dma((PAIRS,)), dma((PAIRS,)),
            dma((PAIRS, 4, 2)), dma((PAIRS, 4, 2)),
            dma((PAIRS, 7)), dma((PAIRS, 7)),
            dma((PAIRS, 4, 2)), dma((PAIRS, 4, 2)),
            dma((PAIRS, 5)), dma((PAIRS, 5)),
            dma((PAIRS, 5, 2)), dma((PAIRS, 5, 2)),
            dma((PAIRS, 5, 3)), dma((PAIRS, 5, 3)),
            dma((PAIRS, 4)), dma((PAIRS, 4)),
        ],
        compiler_params=pltpu.CompilerParams(collective_id=0, has_side_effects=True, vmem_limit_bytes=63 << 20),
    )(queries, keys, values)


def solution(mesh):
    spec = P("seq", "res", None)
    return jax.shard_map(local, mesh=mesh, in_specs=(spec, spec, spec), out_specs=spec, check_vma=False)
```
